32 devices in a mesh: seq: 4 (over z), dp: 2 (over core), head: 4 (over y, x).
Axes of the slice: x: 2, y: 2, z: 4, core: 2. Of those that a mesh axis runs over, the one named last changes fastest.
Arguments:
- hidden_in: bfloat16 [16, 1024, 1024], P('dp', 'seq', 'head'), may hold values from -6 to 6
- norm_gain: bfloat16 [1024], P('head'), may hold values from 0.5 to 1.5
- w_z: bfloat16 [1024, 2048], P(None, 'head'), may hold values from -0.1875 to 0.1875
- w_x: bfloat16 [1024, 2048], P(None, 'head'), may hold values from -0.1875 to 0.1875
- w_bc: bfloat16 [1024, 256], P(None, 'head'), may hold values from -0.1875 to 0.1875
- w_dt: bfloat16 [1024, 32], P(None, 'head'), may hold values from -0.1875 to 0.1875
- conv_x: float32 [4, 2048], P(None, 'head'), may hold values from -0.5 to 0.5
- conv_x_bias: float32 [2048], P('head'), may hold values from -0.5 to 0.5
- conv_bc: float32 [4, 256], P(None, 'head'), may hold values from -0.5 to 0.5
- conv_bc_bias: float32 [256], P('head'), may hold values from -0.5 to 0.5
- dt_bias: float32 [32], P('head'), may hold values from -3.5 to -2.5
- a_log: float32 [32], P('head'), may hold values from -8 to 0
- skip: float32 [32], P('head'), may hold values from 0.5 to 1.5
- gate_gain: float32 [2048], P('head'), may hold values from 0.5 to 1.5
- w_out: bfloat16 [2048, 1024], P('head'), may hold values from -0.1875 to 0.1875
- out_grad: bfloat16 [16, 1024, 1024], P('dp', 'seq', 'head'), may hold values from -6 to 6
Outputs:
- block_out: bfloat16 [16, 1024, 1024], P('dp', 'seq', 'head')
- grad_in: float32 [16, 1024, 1024], P('dp', 'seq', 'head')
- grad_norm_gain: float32 [1024], P('head')
- grad_w_z: float32 [1024, 2048], P(None, 'head')
- grad_w_x: float32 [1024, 2048], P(None, 'head')
- grad_w_bc: float32 [1024, 256], P(None, 'head')
- grad_w_dt: float32 [1024, 32], P(None, 'head')
- grad_conv_x: float32 [4, 2048], P(None, 'head')
- grad_conv_x_bias: float32 [2048], P('head')
- grad_conv_bc: float32 [4, 256], P(None, 'head')
- grad_conv_bc_bias: float32 [256], P('head')
- grad_dt_bias: float32 [32], P('head')
- grad_a_log: float32 [32], P('head')
- grad_skip: float32 [32], P('head')
- grad_gate_gain: float32 [2048], P('head')
- grad_w_out: float32 [2048, 1024], P('head')
The draws below stay inside these ranges and needn't reach their ends.
All inputs are finite; a program needn't handle non-finite values.
Results may differ from the reference program's by a relative error of at most 0.0025.
The reference program's roundings to bfloat16 on the way (of `normed` and `scaled`) count: a program that leaves them out, or rounds other values in their place, can miss the bound.
Values may be sent and summed in bfloat16 or wider, within the bound.
No kernel may reach another device: no remote copies, remote signals or barrier semaphores. Data moves between devices by JAX's collectives and lax.ppermute only.
A program may use at most 320 MiB of HBM per device.

```python
import math
import jax
import jax.numpy as jnp
from jax import lax

D = 1024
DI = 2048
HEADS = 32
HEAD_DIM = 64
STATE = 128
CONV = 4
LENGTH = 1024
SEQS = 16


def draw_a_log(key, part):
    key = jax.random.fold_in(key, 7)
    key_kind, key_slow, key_fast = jax.random.split(key, 3)
    slow_share = 0.5
    slow_heads = jax.random.bernoulli(key_kind, slow_share, (HEADS,))
    slow_level = jax.random.uniform(key_slow, (HEADS,), jnp.float32, 0.3, 1.5)
    fast_level = jax.random.uniform(key_fast, (HEADS,), jnp.float32, 0.7, 1.5)
    reach = max(0.08 * LENGTH, 2.0)
    slow_value = jnp.log(slow_level / reach)
    fast_value = jnp.log(0.3 * fast_level)
    return jnp.where(slow_heads, slow_value, fast_value).astype(jnp.float32)


def with_spikes(entries, own_key, source, target, blocks, factor):
    owner, partner = [(jnp.arange(entries.shape[dim]) // (entries.shape[dim] // blocks)).reshape([-1 if axis == dim else 1 for axis in range(entries.ndim)]) for dim in (source, target)]
    chosen = jax.random.permutation(own_key, blocks)[partner]
    strong = (owner == chosen) | (owner == (partner + blocks // 2) % blocks)
    return jnp.where(strong, factor * entries, entries)


def shard_levels(rng, dims, cuts, least, largest):
    gain = 1.0
    for axis_at, shards_of in cuts:
        draws = jax.random.uniform(jax.random.fold_in(jax.random.fold_in(rng, 6), axis_at), (shards_of,), jnp.float32, least / len(cuts), largest / len(cuts))
        gain = gain * jnp.repeat(jnp.exp(draws), dims[axis_at] // shards_of).reshape((-1,) + (1,) * (len(dims) - 1 - axis_at))
    return gain


def centred(key, shape, scale, most, shards=(), kind=jnp.bfloat16):
    values = scale * jax.random.normal(key, shape, jnp.float32)
    if shards:
        values = values * shard_levels(key, shape, shards, -0.22, 0.18)
    return jnp.clip(values, -most, most).astype(kind)


def heavy_noise(own_key, dims, scale, most, shards, heavy, kind=jnp.bfloat16):
    entries = scale * jax.random.normal(own_key, dims, jnp.float32)
    if shards:
        entries = entries * shard_levels(own_key, dims, shards, -0.22, 0.18)
    return jnp.clip(with_spikes(entries, jax.random.fold_in(own_key, 3), *heavy), -most, most).astype(kind)


def setup_inputs(seed: int = 0) -> dict:
    keys = jax.random.split(jax.random.key(seed), 17)
    hidden_in = centred(keys[0], (SEQS, LENGTH, D), 1.0, 6.0, ((0, 2), (1, 4), (2, 4)))
    norm_gain = jnp.clip(1.0 + 0.1 * jax.random.normal(keys[1], (D,), jnp.float32), 0.5, 1.5).astype(jnp.bfloat16)
    w_z = centred(keys[2], (D, DI), D ** -0.5, 0.1875, ((1, 4),))
    w_x = centred(keys[3], (D, DI), D ** -0.5, 0.1875, ((1, 4),))
    w_bc = centred(keys[4], (D, 2 * STATE), D ** -0.5, 0.1875, ((1, 4),))
    w_dt = centred(keys[5], (D, HEADS), D ** -0.5, 0.1875, ((1, 4),))
    conv_x = jnp.clip(jax.random.uniform(keys[6], (CONV, DI), jnp.float32, -0.5, 0.5) * shard_levels(keys[6], (CONV, DI), ((1, 4),), -0.4, 0.0), -0.5, 0.5)
    conv_x_bias = jnp.clip(jax.random.uniform(keys[7], (DI,), jnp.float32, -0.5, 0.5) * shard_levels(keys[7], (DI,), ((0, 4),), -0.4, 0.0), -0.5, 0.5)
    conv_bc = jnp.clip(jax.random.uniform(keys[8], (CONV, 2 * STATE), jnp.float32, -0.5, 0.5) * shard_levels(keys[8], (CONV, 2 * STATE), ((1, 4),), -0.4, 0.0), -0.5, 0.5)
    conv_bc_bias = jnp.clip(jax.random.uniform(keys[9], (2 * STATE,), jnp.float32, -0.5, 0.5) * shard_levels(keys[9], (2 * STATE,), ((0, 4),), -0.4, 0.0), -0.5, 0.5)
    dt_bias = jnp.clip(-3.5 + 1.0 * jax.random.uniform(keys[10], (HEADS,), jnp.float32) ** shard_levels(keys[10], (HEADS,), ((0, 4),), -0.2, 0.2), -3.5, -2.5)
    a_log = draw_a_log(jax.random.fold_in(keys[16], 71), 0)
    skip = jnp.clip(0.5 + 1.0 * jax.random.uniform(keys[12], (HEADS,), jnp.float32) ** shard_levels(keys[12], (HEADS,), ((0, 4),), -0.2, 0.2), 0.5, 1.5)
    gate_gain = jnp.clip(1.0 + 0.1 * jax.random.normal(keys[13], (DI,), jnp.float32), 0.5, 1.5)
    w_out = heavy_noise(keys[14], (DI, D), DI ** -0.5, 0.1875, ((0, 4),), (0, 1, 4, 2.0))
    out_grad = centred(keys[15], (SEQS, LENGTH, D), 1.0, 6.0, ((0, 2), (1, 4), (2, 4)))
    return dict(hidden_in=hidden_in, norm_gain=norm_gain, w_z=w_z, w_x=w_x, w_bc=w_bc, w_dt=w_dt, conv_x=conv_x, conv_x_bias=conv_x_bias, conv_bc=conv_bc, conv_bc_bias=conv_bc_bias, dt_bias=dt_bias, a_log=a_log, skip=skip, gate_gain=gate_gain, w_out=w_out, out_grad=out_grad)


epsilon = 1e-05
highest = lax.Precision.HIGHEST

@jax.custom_vjp
def low(v):
    return lax.optimization_barrier(v.astype(jnp.bfloat16)).astype(jnp.float32)

@jax.custom_vjp
def low_back(v):
    return v

def low_keep(v):
    return (low(v), None)

def low_pass(kept, grad):
    return (grad,)

def back_keep(v):
    return (v, None)

def back_low(kept, grad):
    return (low(grad),)
low.defvjp(low_keep, low_pass)
low_back.defvjp(back_keep, back_low)

def causal_conv(values, kernel, kernel_bias):
    kernel_span = kernel.shape[0]
    length = values.shape[1]
    padded = jnp.pad(values, ((0, 0), (kernel_span - 1, 0), (0, 0)))
    result = kernel_bias + jnp.zeros_like(values)
    for tap_index in range(kernel_span):
        result = result + kernel[tap_index] * padded[:, tap_index:tap_index + length]
    return result

def ssd_block(carried, block_data):
    inputs, b_rows, c_rows, step_size, step_log = block_data
    cumulative = jnp.cumsum(step_log, axis=1)
    extent = cumulative.shape[1]
    causal = (jnp.arange(extent)[:, None] >= jnp.arange(extent)[None, :])[None, :, :, None]
    gap_log = cumulative[:, :, None, :] - cumulative[:, None, :, :]
    decay_mat = jnp.where(causal, jnp.exp(jnp.where(causal, gap_log, 0.0)), 0.0)
    scores = jnp.einsum('gtn,gsn->gts', c_rows, b_rows, precision=highest)
    weights = scores[..., None] * decay_mat * step_size[:, None, :, :]
    output = jnp.einsum('gtsh,gshp->gthp', weights, inputs, precision=highest)
    output = output + jnp.exp(cumulative)[..., None] * jnp.einsum('gtn,ghpn->gthp', c_rows, carried, precision=highest)
    last_log = cumulative[:, -1, :]
    carry_weight = jnp.exp(last_log[:, None, :] - cumulative) * step_size
    carried = jnp.exp(last_log)[:, :, None, None] * carried + jnp.einsum('gshp,gsn->ghpn', inputs * carry_weight[..., None], b_rows, precision=highest)
    return (carried, output)

def scan_states(inputs, b_rows, c_rows, step_size, step_log):
    per_group, length = (inputs.shape[0], inputs.shape[1])
    extent = math.gcd(length, 256)
    block_count = length // extent

    def blocks(array):
        shaped = array.reshape((per_group, block_count, extent) + array.shape[2:])
        return jnp.moveaxis(shaped, 1, 0)
    initial = jnp.zeros((per_group, inputs.shape[2], inputs.shape[3], b_rows.shape[2]), jnp.float32)
    _, outputs = lax.scan(jax.checkpoint(ssd_block), initial, (blocks(inputs), blocks(b_rows), blocks(c_rows), blocks(step_size), blocks(step_log)))
    return jnp.moveaxis(outputs, 0, 1).reshape(inputs.shape)

def project(left_side, matrix):
    return jnp.einsum('gld,de->gle', left_side, matrix, precision=highest)

def forward(tokens, norm_gain, w_z, w_x, w_bc, w_dt, conv_x, conv_x_bias, conv_bc, conv_bc_bias, dt_bias, a_log, skip, gate_gain, w_out):
    inv_rms = lax.rsqrt(lax.optimization_barrier(jnp.mean(tokens * tokens, axis=-1, keepdims=True)) + epsilon)
    normed = low(tokens * inv_rms * norm_gain)
    gate_pre = low_back(project(normed, w_z))
    x_pre = low_back(project(normed, w_x))
    bc_pre = low_back(project(normed, w_bc))
    dt_raw = low_back(project(normed, w_dt))
    x_conv = low(jax.nn.silu(causal_conv(x_pre, conv_x, conv_x_bias)))
    bc_conv = low(jax.nn.silu(causal_conv(bc_pre, conv_bc, conv_bc_bias)))
    step_size = jax.nn.softplus(dt_raw + dt_bias)
    step_log = step_size * -jnp.exp(a_log)
    shaped = x_conv.reshape(x_conv.shape[:2] + (HEADS, HEAD_DIM))
    ssd_out = scan_states(shaped, bc_conv[..., :STATE], bc_conv[..., STATE:], step_size, step_log)
    ssd_out = (ssd_out + skip[:, None] * shaped).reshape(x_conv.shape)
    gated_out = ssd_out * jax.nn.silu(gate_pre)
    gate_rms = lax.rsqrt(lax.optimization_barrier(jnp.mean(gated_out * gated_out, axis=-1, keepdims=True)) + epsilon)
    scaled = low(gated_out * gate_rms * gate_gain)
    return tokens + project(scaled, w_out)

def reference(hidden_in, norm_gain, w_z, w_x, w_bc, w_dt, conv_x, conv_x_bias, conv_bc, conv_bc_bias, dt_bias, a_log, skip, gate_gain, w_out, out_grad):
    params = tuple((parameter.astype(jnp.float32) for parameter in (norm_gain, w_z, w_x, w_bc, w_dt, conv_x, conv_x_bias, conv_bc, conv_bc_bias, dt_bias, a_log, skip, gate_gain, w_out)))
    per_group = math.gcd(SEQS, max(1, 4096 // LENGTH))
    group_count = SEQS // per_group
    tokens = hidden_in.astype(jnp.float32).reshape(group_count, per_group, LENGTH, D)
    cotangent = out_grad.astype(jnp.float32).reshape(group_count, per_group, LENGTH, D)

    def one_group(totals, group_item):
        group_in, group_cot = group_item
        result, pull_back = jax.vjp(forward, group_in, *params)
        gradients = pull_back(group_cot)
        summed = tuple((earlier + addend for earlier, addend in zip(totals, gradients[1:])))
        return (summed, (result, gradients[0]))
    initial = tuple((jnp.zeros_like(parameter) for parameter in params))
    totals, (results, input_grads) = lax.scan(one_group, initial, (tokens, cotangent))
    block_out = results.reshape(SEQS, LENGTH, D).astype(jnp.bfloat16)
    grad_in = input_grads.reshape(SEQS, LENGTH, D)
    return (block_out, grad_in, totals[0], totals[1], totals[2], totals[3], totals[4], totals[5], totals[6], totals[7], totals[8], totals[9], totals[10], totals[11], totals[12], totals[13])
```

```python
import functools
import jax
import jax.numpy as jnp
from jax import lax
from jax.experimental import pallas as pl
from jax.experimental.pallas import tpu as pltpu
from jax.sharding import PartitionSpec as P

HEAD_DIM = 64
STATE = 128


epsilon = 1e-05
highest = lax.Precision.HIGHEST


def from_behind(value, axis, steps):
    count = lax.axis_size(axis)
    leading, last = (max(0, -steps), min(count, count - steps))
    return lax.ppermute(value, axis, [(source, source + steps) for source in range(leading, last)])


def prefix(value, axis, join, neutral, backward):
    count, mine = (lax.axis_size(axis), lax.axis_index(axis))
    pieces = jax.tree.map(lambda part: lax.all_gather(part, axis), value)
    if backward:
        pieces = jax.tree.map(lambda part: part[::-1], pieces)
        mine = count - 1 - mine
    total = jax.tree.map(
        lambda part, zero: jnp.full_like(part, 0) + jnp.asarray(zero, part.dtype), value, neutral
    )

    def turn(position, total):
        longer = join(total, jax.tree.map(lambda part: part[position], pieces))
        return jax.tree.map(lambda new, old: jnp.where(position < mine, new, old), longer, total)

    return lax.fori_loop(0, count - 1, turn, total)


def silu_grad(pre_value):
    gate_sig = jax.nn.sigmoid(pre_value)
    return gate_sig * (1.0 + pre_value * (1.0 - gate_sig))


def chain_step(earlier, later):
    return (earlier[0] + later[0], earlier[1] * jnp.exp(later[0])[:, :, None, None] + later[1])


def on_device_general(
    hidden_in,
    norm_gain,
    w_z,
    w_x,
    w_bc,
    w_dt,
    conv_x,
    conv_x_bias,
    conv_bc,
    conv_bc_bias,
    dt_bias,
    a_log,
    skip,
    gate_gain,
    w_out,
    out_grad,
):
    seq_count, local_len, part_width = hidden_in.shape
    heads_here = dt_bias.shape[0]
    inner_here = w_x.shape[1]
    bc_here = w_bc.shape[1]
    kernel_span = conv_x.shape[0]
    edge_len = kernel_span - 1
    row_count = seq_count * local_len
    whole_x, whole_cot, whole_gain = (
        lax.all_gather(hidden_in, "head", axis=2, tiled=True),
        lax.all_gather(out_grad, "head", axis=2, tiled=True),
        lax.all_gather(norm_gain, "head", axis=0, tiled=True),
    )
    full_width = whole_x.shape[2]
    x_full = whole_x.astype(jnp.float32)
    inv_rms = lax.rsqrt(jnp.mean(x_full * x_full, axis=-1, keepdims=True) + epsilon)
    normed = (
        (x_full * inv_rms * whole_gain.astype(jnp.float32))
        .astype(jnp.bfloat16)
        .reshape(row_count, full_width)
    )
    w_cat = jnp.concatenate([w_z, w_x, w_bc, w_dt], axis=1)
    projected = jnp.dot(normed, w_cat, preferred_element_type=jnp.float32).reshape(
        seq_count, local_len, -1
    )
    conv_end = 2 * inner_here + bc_here
    gate_pre = projected[:, :, :inner_here]
    conv_in = projected[:, :, inner_here:conv_end]
    dt_raw = projected[:, :, conv_end:]
    edge_in = from_behind(conv_in[:, local_len - edge_len :, :], "seq", 1)
    extended = jnp.concatenate([edge_in, conv_in], axis=1)
    kernel = jnp.concatenate([conv_x, conv_bc], axis=1)
    kernel_bias = jnp.concatenate([conv_x_bias, conv_bc_bias], axis=0)
    pre_act = jnp.broadcast_to(kernel_bias, conv_in.shape)
    for tap_index in range(kernel_span):
        pre_act = pre_act + kernel[tap_index] * extended[:, tap_index : tap_index + local_len]
    activated = jax.nn.silu(pre_act)
    x_conv = activated[:, :, :inner_here].astype(jnp.bfloat16)
    bc_all = lax.all_gather(
        activated[:, :, inner_here:].astype(jnp.bfloat16), "head", axis=2, tiled=True
    )
    b_rows = bc_all[:, :, :STATE].astype(jnp.float32)
    c_rows = bc_all[:, :, STATE:].astype(jnp.float32)
    values = x_conv.astype(jnp.float32).reshape(seq_count, local_len, heads_here, HEAD_DIM)
    step_size = jax.nn.softplus(dt_raw + dt_bias)
    decay_rate = -jnp.exp(a_log)
    step_log = step_size * decay_rate
    cumulative = jnp.cumsum(step_log, axis=1)
    total_log = cumulative[:, -1, :]
    cum_heads = cumulative.transpose(0, 2, 1)
    step_heads = step_size.transpose(0, 2, 1)
    causal = jnp.arange(local_len)[:, None] >= jnp.arange(local_len)[None, :]
    gap_log = cum_heads[:, :, :, None] - cum_heads[:, :, None, :]
    decay_mat = jnp.where(causal, jnp.exp(jnp.where(causal, gap_log, 0.0)), 0.0)
    scores = jnp.einsum("btn,bsn->bts", c_rows, b_rows, precision=highest)
    decayed = scores[:, None, :, :] * decay_mat
    weights = decayed * step_heads[:, :, None, :]
    local_out = jnp.einsum("bhts,bshp->bthp", weights, values, precision=highest)
    carry_scale = jnp.exp(total_log[:, None, :] - cumulative)
    carry_weight = carry_scale * step_size
    weighted_values = values * carry_weight[..., None]
    local_state = jnp.einsum("bshp,bsn->bhpn", weighted_values, b_rows, precision=highest)
    empty = (jnp.zeros_like(total_log), jnp.zeros_like(local_state))
    _, state_in = prefix((total_log, local_state), "seq", chain_step, empty, False)
    cum_exp = jnp.exp(cumulative)
    cross_out = cum_exp[..., None] * jnp.einsum(
        "btn,bhpn->bthp", c_rows, state_in, precision=highest
    )
    ssd_out = (local_out + cross_out + skip[:, None] * values).reshape(
        seq_count, local_len, inner_here
    )
    gate_act = jax.nn.silu(gate_pre)
    gated_out = ssd_out * gate_act
    inner_width = inner_here * lax.axis_size("head")
    square_sum = lax.psum(jnp.sum(gated_out * gated_out, axis=-1), "head")
    gate_rms = lax.rsqrt(square_sum / inner_width + epsilon)[..., None]
    scaled = (gated_out * gate_rms * gate_gain).astype(jnp.bfloat16).reshape(row_count, inner_here)
    out_own = lax.psum_scatter(
        lax.dot_general(
            w_out, scaled, (((0,), (1,)), ((), ())), preferred_element_type=jnp.float32
        ),
        "head",
        scatter_dimension=0,
        tiled=True,
    )
    x_own = hidden_in.astype(jnp.float32)
    block_out = (x_own + out_own.T.reshape(seq_count, local_len, part_width)).astype(jnp.bfloat16)
    cot_rows = whole_cot.reshape(row_count, full_width)
    g_w_out = lax.dot_general(
        scaled, cot_rows, (((0,), (0,)), ((), ())), preferred_element_type=jnp.float32
    )
    d_scaled = lax.dot_general(
        cot_rows, w_out, (((1,), (1,)), ((), ())), preferred_element_type=jnp.float32
    )
    d_scaled = d_scaled.reshape(seq_count, local_len, inner_here)
    g_gate_gain = jnp.sum(d_scaled * gated_out * gate_rms, axis=(0, 1))
    gain_term = d_scaled * gate_gain
    inner_dot = lax.psum(jnp.sum(gain_term * gated_out, axis=-1), "head")
    d_gated = gate_rms * gain_term - gated_out * gate_rms**3 * (inner_dot / inner_width)[..., None]
    d_gate = d_gated * ssd_out * silu_grad(gate_pre)
    d_out = (d_gated * gate_act).reshape(seq_count, local_len, heads_here, HEAD_DIM)
    g_skip = jnp.sum(d_out * values, axis=(0, 1, 3))
    gram = jnp.einsum("bthp,bshp->bhts", d_out, values, precision=highest)
    d_values = (
        jnp.einsum("bhts,bthp->bshp", weights, d_out, precision=highest) + skip[:, None] * d_out
    )
    masked = gram * decayed
    d_scores = jnp.sum(gram * decay_mat * step_heads[:, :, None, :], axis=1)
    d_step_intra = jnp.sum(masked, axis=2).transpose(0, 2, 1)
    d_gap = masked * step_heads[:, :, None, :]
    d_cum_intra = (jnp.sum(d_gap, axis=3) - jnp.sum(d_gap, axis=2)).transpose(0, 2, 1)
    d_c = jnp.einsum("bts,bsn->btn", d_scores, b_rows, precision=highest)
    d_b = jnp.einsum("bts,btn->bsn", d_scores, c_rows, precision=highest)
    d_out_exp = d_out * cum_exp[..., None]
    d_c = d_c + jnp.einsum("bthp,bhpn->btn", d_out_exp, state_in, precision=highest)
    d_state_in = jnp.einsum("bthp,btn->bhpn", d_out_exp, c_rows, precision=highest)
    d_cum_cross = jnp.sum(d_out * cross_out, axis=3)
    _, d_local_state = prefix((total_log, d_state_in), "seq", chain_step, empty, True)
    state_back = jnp.einsum("bhpn,bsn->bshp", d_local_state, b_rows, precision=highest)
    d_values = d_values + carry_weight[..., None] * state_back
    d_b = d_b + jnp.einsum("bshp,bhpn->bsn", weighted_values, d_local_state, precision=highest)
    d_carry = jnp.sum(values * state_back, axis=3)
    carry_prod = d_carry * carry_weight
    d_total = jnp.exp(total_log) * jnp.sum(state_in * d_local_state, axis=(2, 3)) + jnp.sum(
        carry_prod, axis=1
    )
    d_cum = d_cum_intra + d_cum_cross - carry_prod
    d_cum = d_cum.at[:, -1, :].add(d_total)
    d_step_log = jnp.cumsum(d_cum[:, ::-1, :], axis=1)[:, ::-1, :]
    d_step = d_step_intra + d_carry * carry_scale + d_step_log * decay_rate
    g_a_log = jnp.sum(d_step_log * step_log, axis=(0, 1))
    d_dt_pre = d_step * jax.nn.sigmoid(dt_raw + dt_bias)
    g_dt_bias = jnp.sum(d_dt_pre, axis=(0, 1))
    d_bc_own = lax.psum_scatter(
        jnp.concatenate([d_b, d_c], axis=2), "head", scatter_dimension=2, tiled=True
    )
    d_act = jnp.concatenate([d_values.reshape(seq_count, local_len, inner_here), d_bc_own], axis=2)
    d_pre = d_act * silu_grad(pre_act)
    g_kernel = jnp.stack(
        [
            jnp.sum(d_pre * extended[:, tap_index : tap_index + local_len], axis=(0, 1))
            for tap_index in range(kernel_span)
        ]
    )
    g_kernel_bias = jnp.sum(d_pre, axis=(0, 1))
    d_padded = jnp.pad(d_pre, ((0, 0), (edge_len, edge_len), (0, 0)))
    d_ext = jnp.zeros_like(extended)
    for tap_index in range(kernel_span):
        offset = edge_len - tap_index
        d_ext = d_ext + kernel[tap_index] * d_padded[:, offset : offset + local_len + edge_len]
    back_edge = from_behind(d_ext[:, :edge_len, :], "seq", -1)
    d_conv_in = d_ext[:, edge_len:, :].at[:, local_len - edge_len :, :].add(back_edge)
    d_proj = (
        jnp.concatenate([d_gate, d_conv_in, d_dt_pre], axis=2)
        .astype(jnp.bfloat16)
        .reshape(row_count, -1)
    )
    g_w_cat = lax.dot_general(
        normed, d_proj, (((0,), (0,)), ((), ())), preferred_element_type=jnp.float32
    )
    x_hat_own = x_own * inv_rms
    gain_own = norm_gain.astype(jnp.float32)
    d_own = lax.psum_scatter(
        lax.dot_general(
            w_cat, d_proj, (((1,), (1,)), ((), ())), preferred_element_type=jnp.float32
        ),
        "head",
        scatter_dimension=0,
        tiled=True,
    ).T.reshape(seq_count, local_len, part_width)
    d_hat_own = d_own * gain_own
    row_mean = lax.psum(jnp.sum(d_hat_own * x_hat_own, axis=-1), "head")[..., None] / full_width
    grad_in = out_grad.astype(jnp.float32) + inv_rms * (d_hat_own - x_hat_own * row_mean)
    g_norm_gain = jnp.sum(d_own * x_hat_own, axis=(0, 1))
    (
        g_norm_gain,
        g_w_cat,
        g_kernel,
        g_kernel_bias,
        g_dt_bias,
        g_a_log,
        g_skip,
        g_gate_gain,
        g_w_out,
    ) = lax.psum(
        (
            g_norm_gain,
            g_w_cat,
            g_kernel,
            g_kernel_bias,
            g_dt_bias,
            g_a_log,
            g_skip,
            g_gate_gain,
            g_w_out,
        ),
        ("seq", "dp"),
    )
    g_w_z = g_w_cat[:, :inner_here]
    g_w_x = g_w_cat[:, inner_here : 2 * inner_here]
    g_w_bc = g_w_cat[:, 2 * inner_here : conv_end]
    g_w_dt = g_w_cat[:, conv_end:]
    return (
        block_out,
        grad_in,
        g_norm_gain,
        g_w_z,
        g_w_x,
        g_w_bc,
        g_w_dt,
        g_kernel[:, :inner_here],
        g_kernel_bias[:inner_here],
        g_kernel[:, inner_here:],
        g_kernel_bias[inner_here:],
        g_dt_bias,
        g_a_log,
        g_skip,
        g_gate_gain,
        g_w_out,
    )


BF = jnp.bfloat16
F32 = jnp.float32
CHUNK = 256
LANES = 128
VMEM_LIMIT = 56 * 1024 * 1024


def dot_nn(a, b):
    return lax.dot_general(a, b, (((1,), (0,)), ((), ())), preferred_element_type=F32)


def dot_nt(a, b):
    return lax.dot_general(a, b, (((1,), (1,)), ((), ())), preferred_element_type=F32)


def dot_tn(a, b):
    return lax.dot_general(a, b, (((0,), (0,)), ((), ())), preferred_element_type=F32)


def split2(value):
    high = value.astype(BF)
    return high, (value - high.astype(F32)).astype(BF)


def split3(value):
    high = value.astype(BF)
    rest = value - high.astype(F32)
    middle = rest.astype(BF)
    return high, middle, (rest - middle.astype(F32)).astype(BF)


def sigmoid(value):
    return 1.0 / (1.0 + jnp.exp(-value))


def silu_slope(value, sig):
    return sig * (1.0 + value * (1.0 - sig))


def step_values(dt_block, dt_params):
    shifted = dt_block + dt_params[0:1]
    step = jnp.maximum(shifted, 0.0) + jnp.log1p(jnp.exp(-jnp.abs(shifted)))
    rate = -jnp.exp(dt_params[1:2])
    return shifted, step, rate, step * rate


def inverse_rms(blocks):
    total = sum(jnp.sum(block * block, axis=1, keepdims=True) for block in blocks)
    return lax.rsqrt(total / (len(blocks) * blocks[0].shape[1]) + epsilon)


def normed_blocks(x_refs, gain_ref):
    blocks = [ref[...].astype(F32) for ref in x_refs]
    inverse = inverse_rms(blocks)
    hats = [block * inverse for block in blocks]
    return inverse, hats, [(hat * gain_ref[k : k + 1]).astype(BF) for k, hat in enumerate(hats)]


def block_of(index_ref, k, size):
    return pl.ds(pl.multiple_of(index_ref[k] * size, size), size)


def column_of_sums(rows, lanes_here):
    tile = jnp.zeros((CHUNK, LANES), F32)
    lane = lax.broadcasted_iota(jnp.int32, (CHUNK, LANES), 1)
    for position, value in enumerate(rows):
        tile = jnp.where(lane == position, value, tile)
    return jnp.transpose(tile)[0:lanes_here]


def forward_kernel(
    index_ref, x0, x1, x2, x3, w_ref, gain_ref, taps_ref, dt_ref, skip_ref, spread_ref, lower_ref,
    gate_out, conv_out, ssd_out, state_out, extended, state,
):
    inner = skip_ref.shape[1]
    heads = inner // HEAD_DIM
    conv_width = inner + 2 * STATE

    @pl.when(pl.program_id(0) == 0)
    def _():
        extended[0:8, :] = jnp.zeros((8, conv_width), F32)
        state[...] = jnp.zeros(state.shape, F32)

    x_refs = (x0, x1, x2, x3)
    _, _, normed = normed_blocks(x_refs, gain_ref)
    projected = sum(
        dot_nn(part, w_ref[block_of(index_ref, k, part.shape[1]), :])
        for k, part in enumerate(normed)
    )
    gate_out[...] = projected[:, :inner]
    conv_out[...] = projected[:, inner:]
    conv_in = projected[:, inner : inner + conv_width]
    extended[8 : 8 + CHUNK, :] = conv_in
    pre_act = taps_ref[4:5, :] + taps_ref[3:4, :] * conv_in
    for k in range(3):
        pre_act = pre_act + taps_ref[k : k + 1, :] * extended[5 + k : 5 + k + CHUNK, :]
    extended[0:8, :] = conv_in[CHUNK - 8 :, :]
    act = (pre_act * sigmoid(pre_act)).astype(BF)
    values = act[:, :inner]
    b_rows = act[:, inner : inner + STATE]
    c_rows = act[:, inner + STATE :]

    _, step, _, step_log = step_values(projected[:, inner + conv_width :], dt_ref)
    cumulative = sum(dot_nn(lower_ref[...], part) for part in split3(step_log))
    cum_t = jnp.transpose(cumulative)
    step_t = jnp.transpose(step)
    total = cumulative[CHUNK - 1 : CHUNK, :]
    spread = spread_ref[...]
    widened = jnp.concatenate([jnp.exp(cumulative), jnp.exp(total - cumulative) * step], axis=0)
    high, low = split2(widened)
    widened = dot_nn(high, spread) + dot_nn(low, spread)
    cum_exp, carry_weight = widened[:CHUNK], widened[CHUNK:]

    state_now = state[...]
    state_out[...] = state_now
    s_high, s_low = split2(state_now)
    cross = dot_nt(c_rows, s_high) + dot_nt(c_rows, s_low)
    values_f = values.astype(F32)
    carried = cum_exp * cross + skip_ref[...] * values_f

    scores = dot_nt(c_rows, b_rows)
    row = lax.broadcasted_iota(jnp.int32, (CHUNK, CHUNK), 0)
    column = lax.broadcasted_iota(jnp.int32, (CHUNK, CHUNK), 1)
    causal = row >= column
    lane = lax.broadcasted_iota(jnp.int32, (CHUNK, LANES), 1)
    for pair in range(heads // 2):
        lanes = slice(pair * LANES, (pair + 1) * LANES)
        total_out = carried[:, lanes]
        for side in range(2):
            h = 2 * pair + side
            mine = (lane >= HEAD_DIM) if side else (lane < HEAD_DIM)
            own_values = jnp.where(mine, values[:, lanes], jnp.zeros((), BF))
            gap = cumulative[:, h : h + 1] - cum_t[h : h + 1, :]
            decay = jnp.exp(jnp.where(causal, gap, -1e30))
            high, low = split2(scores * decay * step_t[h : h + 1, :])
            total_out = total_out + dot_nn(high, own_values) + dot_nn(low, own_values)
        ssd_out[:, lanes] = total_out

    high, low = split2(values_f * carry_weight)
    grown = dot_tn(high, b_rows) + dot_tn(low, b_rows)
    total_t = jnp.exp(cum_t[:, CHUNK - 1 : CHUNK])
    for h in range(heads):
        part = slice(h * HEAD_DIM, (h + 1) * HEAD_DIM)
        state[part, :] = total_t[h : h + 1, :] * state_now[part] + grown[part]


def score_kernel(index_ref, g0, g1, g2, g3, w_ref, ssd_ref, gate_ref, gain_ref, d_out, sums_out):
    d_scaled = sum(
        dot_nn(ref[...], w_ref[block_of(index_ref, k, ref.shape[1]), :])
        for k, ref in enumerate((g0, g1, g2, g3))
    )
    d_out[...] = d_scaled
    gate = gate_ref[...]
    gated = ssd_ref[...] * (gate * sigmoid(gate))
    squares = jnp.sum(gated * gated, axis=1, keepdims=True)
    inner_dot = jnp.sum(d_scaled * gain_ref[...] * gated, axis=1, keepdims=True)
    sums_out[0] = column_of_sums((squares, inner_dot), 8)


def backward_kernel(
    inner_width, index_ref, q0, q1, q2, q3, ssd_ref, gate_ref, d_scaled_ref, conv_ref, before_ref,
    state_ref, gain_ref, taps_ref, dt_ref, skip_ref, spread_ref, gather_ref, lower_ref, upper_ref,
    scaled_out, d_gate_out, d_x_out, d_dt_out, d_bc_out, wide_out, dt_out,
    extended, d_pre, state_grad,
):
    inner = skip_ref.shape[1]
    heads = inner // HEAD_DIM
    conv_width = inner + 2 * STATE
    step_at = pl.program_id(0)
    chunk_at = pl.num_programs(0) - 1 - step_at

    @pl.when(step_at == 0)
    def _():
        d_pre[CHUNK : CHUNK + 8, :] = jnp.zeros((8, inner), F32)
        state_grad[...] = jnp.zeros(state_grad.shape, F32)
        wide_out[...] = jnp.zeros(wide_out.shape, F32)
        dt_out[...] = jnp.zeros(dt_out.shape, F32)

    sums = q0[0] + q1[0] + q2[0] + q3[0]
    sums = jnp.transpose(jnp.concatenate([sums, jnp.zeros((LANES - 8, CHUNK), F32)], axis=0))
    rms = lax.rsqrt(sums[:, 0:1] / inner_width + epsilon)
    mean_dot = sums[:, 1:2] / inner_width
    gate = gate_ref[...]
    gate_sig = sigmoid(gate)
    gate_act = gate * gate_sig
    ssd = ssd_ref[...]
    gated = ssd * gate_act
    gated_rms = gated * rms
    gain = gain_ref[...]
    d_scaled = d_scaled_ref[...]
    scaled_out[...] = (gated_rms * gain).astype(BF)
    wide_out[5:6, :] += jnp.sum(d_scaled * gated_rms, axis=0, keepdims=True)
    d_gated = rms * (d_scaled * gain) - gated * (rms * rms * rms * mean_dot)
    d_gate_out[...] = (d_gated * ssd * silu_slope(gate, gate_sig)).astype(BF)
    d_ssd = d_gated * gate_act

    conv_in = conv_ref[:, :conv_width]
    extended[0:8, :] = jnp.where(chunk_at > 0, before_ref[:, :conv_width], 0.0)
    extended[8 : 8 + CHUNK, :] = conv_in
    pre_act = taps_ref[4:5, :] + taps_ref[3:4, :] * conv_in
    for k in range(3):
        pre_act = pre_act + taps_ref[k : k + 1, :] * extended[5 + k : 5 + k + CHUNK, :]
    sig = sigmoid(pre_act)
    act = (pre_act * sig).astype(BF)
    slope_x = silu_slope(pre_act[:, :inner], sig[:, :inner])
    values = act[:, :inner]
    values_f = values.astype(F32)
    b_rows = act[:, inner : inner + STATE]
    c_rows = act[:, inner + STATE :]
    wide_out[6:7, :] += jnp.sum(d_ssd * values_f, axis=0, keepdims=True)

    shifted, step, rate, step_log = step_values(conv_ref[:, conv_width:], dt_ref)
    cumulative = sum(dot_nn(lower_ref[...], part) for part in split3(step_log))
    cum_t = jnp.transpose(cumulative)
    total = cumulative[CHUNK - 1 : CHUNK, :]
    carry_scale = jnp.exp(total - cumulative)
    carry = carry_scale * step
    spread = spread_ref[...]
    high, low = split2(jnp.concatenate([jnp.exp(cumulative), carry], axis=0))
    widened = dot_nn(high, spread) + dot_nn(low, spread)
    cum_exp, carry_weight = widened[:CHUNK], widened[CHUNK:]

    scores = dot_nt(b_rows, c_rows)
    row = lax.broadcasted_iota(jnp.int32, (CHUNK, CHUNK), 0)
    column = lax.broadcasted_iota(jnp.int32, (CHUNK, CHUNK), 1)
    causal = row <= column
    lane = lax.broadcasted_iota(jnp.int32, (CHUNK, LANES), 1)

    s_high, s_low = split2(state_ref[...])
    r_now = state_grad[...]
    r_high, r_low = split2(r_now)
    cross = cum_exp * (dot_nt(c_rows, s_high) + dot_nt(c_rows, s_low))
    back = dot_nt(b_rows, r_high) + dot_nt(b_rows, r_low)
    d_values = carry_weight * back + skip_ref[...] * d_ssd

    d_scores = jnp.zeros((CHUNK, CHUNK), F32)
    step_intra = jnp.zeros((CHUNK, LANES), F32)
    row_sums = []
    d_parts = []
    for pair in range(heads // 2):
        lanes = slice(pair * LANES, (pair + 1) * LANES)
        g_high, g_low = split2(d_ssd[:, lanes])
        part = d_values[:, lanes]
        for side in range(2):
            h = 2 * pair + side
            mine = (lane >= HEAD_DIM) if side else (lane < HEAD_DIM)
            zero = jnp.zeros((), BF)
            own_values = jnp.where(mine, values[:, lanes], zero)
            own_high = jnp.where(mine, g_high, zero)
            own_low = jnp.where(mine, g_low, zero)
            gram = dot_nt(own_values, g_high) + dot_nt(own_values, g_low)
            gap = cum_t[h : h + 1, :] - cumulative[:, h : h + 1]
            decay = jnp.exp(jnp.where(causal, gap, -1e30))
            step_column = step[:, h : h + 1]
            pulled = gram * decay
            masked = pulled * scores
            d_scores = d_scores + pulled * step_column
            step_intra = jnp.where(
                lane == h, jnp.sum(masked, axis=1, keepdims=True), step_intra
            )
            row_sums.append(jnp.sum(masked * step_column, axis=0, keepdims=True))
            w_high, w_low = split2(scores * decay * step_column)
            part = part + dot_nn(w_high, own_high)
            part = part + dot_nn(w_low, own_high)
            part = part + dot_nn(w_high, own_low)
        d_parts.append(part)
    d_values = jnp.concatenate(d_parts, axis=1)

    high, low = split2(d_scores)
    d_b = dot_nn(high, c_rows) + dot_nn(low, c_rows)
    d_c = dot_tn(high, b_rows) + dot_tn(low, b_rows)
    d_ssd_exp = d_ssd * cum_exp
    e_high, e_low = split2(d_ssd_exp)
    d_c = d_c + dot_nn(e_high, s_high) + dot_nn(e_low, s_high) + dot_nn(e_high, s_low)
    weighted = values_f * carry_weight
    v_high, v_low = split2(weighted)
    d_b = d_b + dot_nn(v_high, r_high) + dot_nn(v_low, r_high) + dot_nn(v_high, r_low)
    d_bc_out[...] = jnp.concatenate([d_b, d_c], axis=1)

    gather = gather_ref[...]
    d_cum_cross = sum(dot_nn(p, gather) for p in split3(d_ssd * cross))
    d_carry = sum(dot_nn(p, gather) for p in split3(values_f * back))
    carry_prod = d_carry * carry
    kept = state_ref[...] * r_now
    kept = sum(dot_tn(gather, p) for p in split3(kept))
    kept = jnp.sum(kept, axis=1, keepdims=True)
    kept = jnp.transpose(jnp.broadcast_to(kept, (LANES, LANES)))[0:1]
    d_total = jnp.exp(total) * kept + jnp.sum(carry_prod, axis=0, keepdims=True)
    rows_t = jnp.concatenate(row_sums + [jnp.zeros((LANES - heads, CHUNK), F32)], axis=0)
    d_cum = jnp.transpose(rows_t) - step * step_intra + d_cum_cross - carry_prod
    last = lax.broadcasted_iota(jnp.int32, (CHUNK, LANES), 0) == CHUNK - 1
    d_cum = d_cum + jnp.where(last, d_total, 0.0)
    d_step_log = sum(dot_nn(upper_ref[...], p) for p in split3(d_cum))
    d_step = step_intra + d_carry * carry_scale + d_step_log * rate
    dt_out[0:1, :] += jnp.sum(d_step_log * step_log, axis=0, keepdims=True)
    d_dt = d_step * sigmoid(shifted)
    dt_out[1:2, :] += jnp.sum(d_dt, axis=0, keepdims=True)
    d_dt_out[...] = d_dt.astype(BF)

    grown = dot_tn(e_high, c_rows) + dot_tn(e_low, c_rows)
    total_t = jnp.exp(cum_t[:, CHUNK - 1 : CHUNK])
    for h in range(heads):
        part = slice(h * HEAD_DIM, (h + 1) * HEAD_DIM)
        state_grad[part, :] = total_t[h : h + 1, :] * r_now[part] + grown[part]

    d_pre_now = d_values * slope_x
    d_pre[0:CHUNK, :] = d_pre_now
    wide_out[4:5, :] += jnp.sum(d_pre_now, axis=0, keepdims=True)
    d_in = taps_ref[3:4, :inner] * d_pre_now
    wide_out[3:4, :] += jnp.sum(d_pre_now * conv_in[:, :inner], axis=0, keepdims=True)
    for k in range(3):
        earlier = extended[5 + k : 5 + k + CHUNK, :inner]
        wide_out[k : k + 1, :] += jnp.sum(d_pre_now * earlier, axis=0, keepdims=True)
        d_in = d_in + taps_ref[k : k + 1, :inner] * d_pre[3 - k : 3 - k + CHUNK, :]
    d_x_out[...] = d_in.astype(BF)
    d_pre[CHUNK : CHUNK + 8, :] = d_pre_now[0:8, :]


def weight_kernel(
    index_ref, x0, x1, x2, x3, gain_ref, w_ref, d_gate_ref, d_x_ref, d_dt_ref,
    d_normed_out, wide_out, dt_out,
):
    @pl.when(pl.program_id(0) == 0)
    def _():
        wide_out[...] = jnp.zeros(wide_out.shape, F32)
        dt_out[...] = jnp.zeros(dt_out.shape, F32)

    _, _, normed = normed_blocks((x0, x1, x2, x3), gain_ref)
    d_wide = jnp.concatenate([d_gate_ref[...], d_x_ref[...]], axis=1)
    d_dt = d_dt_ref[...]
    d_all = jnp.concatenate([d_wide, d_dt], axis=1)
    width = normed[0].shape[1]
    for k, part in enumerate(normed):
        rows = block_of(index_ref, k, width)
        wide_out[rows, :] += dot_tn(part, d_wide)
        dt_out[rows, :] += dot_tn(part, d_dt)
        d_normed_out[:, k * width : (k + 1) * width] = dot_nn(d_all, w_ref[:, rows])


def mixed_kernel(
    index_ref, x0, x1, x2, x3, gain_ref, w_ref, r0, r1, r2, r3, conv_ref, before_ref, taps_ref,
    d_normed_ref, own_out, send1, send2, send3, sums_out, grad_out, taps_out, extended, d_pre,
):
    step_at = pl.program_id(0)
    chunk_at = pl.num_programs(0) - 1 - step_at
    own = conv_ref.shape[1]

    @pl.when(step_at == 0)
    def _():
        d_pre[CHUNK : CHUNK + 8, :] = jnp.zeros((8, own), F32)
        grad_out[...] = jnp.zeros(grad_out.shape, F32)
        taps_out[...] = jnp.zeros(taps_out.shape, F32)

    conv_in = conv_ref[...]
    extended[0:8, :] = jnp.where(chunk_at > 0, before_ref[...], 0.0)
    extended[8 : 8 + CHUNK, :] = conv_in
    pre_act = taps_ref[4:5, :] + taps_ref[3:4, :] * conv_in
    for k in range(3):
        pre_act = pre_act + taps_ref[k : k + 1, :] * extended[5 + k : 5 + k + CHUNK, :]
    d_act = r0[...] + r1[...] + r2[...] + r3[...]
    d_pre_now = d_act * silu_slope(pre_act, sigmoid(pre_act))
    d_pre[0:CHUNK, :] = d_pre_now
    taps_out[4:5, :] += jnp.sum(d_pre_now, axis=0, keepdims=True)
    taps_out[3:4, :] += jnp.sum(d_pre_now * conv_in, axis=0, keepdims=True)
    d_in = taps_ref[3:4, :] * d_pre_now
    for k in range(3):
        earlier = extended[5 + k : 5 + k + CHUNK, :]
        taps_out[k : k + 1, :] += jnp.sum(d_pre_now * earlier, axis=0, keepdims=True)
        d_in = d_in + taps_ref[k : k + 1, :] * d_pre[3 - k : 3 - k + CHUNK, :]
    d_pre[CHUNK : CHUNK + 8, :] = d_pre_now[0:8, :]
    d_in = d_in.astype(BF)

    _, hats, normed = normed_blocks((x0, x1, x2, x3), gain_ref)
    width = normed[0].shape[1]
    row_dot = jnp.zeros((CHUNK, 1), F32)
    for k, out in enumerate((own_out, send1, send2, send3)):
        rows = block_of(index_ref, k, width)
        grad_out[rows, :] += dot_tn(normed[k], d_in)
        d_part = d_normed_ref[:, k * width : (k + 1) * width] + dot_nn(d_in, w_ref[:, rows])
        out[...] = d_part.astype(out.dtype)
        scaled_hat = hats[k] * gain_ref[k : k + 1]
        row_dot = row_dot + jnp.sum(d_part * scaled_hat, axis=1, keepdims=True)
    sums_out[0] = column_of_sums((row_dot,), 8)


def final_kernel(
    x0, x1, x2, x3, gain_ref, own_ref, r1, r2, r3, q0, q1, q2, q3, cot_ref, grad_out, gain_out
):
    @pl.when(pl.program_id(0) == 0)
    def _():
        gain_out[...] = jnp.zeros(gain_out.shape, F32)

    blocks = [ref[...].astype(F32) for ref in (x0, x1, x2, x3)]
    inverse = inverse_rms(blocks)
    hat = blocks[0] * inverse
    sums = q0[0] + q1[0] + q2[0] + q3[0]
    sums = jnp.transpose(jnp.concatenate([sums, jnp.zeros((LANES - 8, CHUNK), F32)], axis=0))
    mean = sums[:, 0:1] / (len(blocks) * hat.shape[1])
    d_own = own_ref[...] + r1[...].astype(F32) + r2[...].astype(F32) + r3[...].astype(F32)
    gain_out[0:1, :] += jnp.sum(d_own * hat, axis=0, keepdims=True)
    d_hat = d_own * gain_ref[0:1]
    grad_out[...] = cot_ref[...].astype(F32) + inverse * (d_hat - hat * mean)


def rows_spec(width, flip=None):
    if flip is None:
        return pl.BlockSpec((CHUNK, width), lambda c: (c, 0))
    return pl.BlockSpec((CHUNK, width), lambda c: (flip - 1 - c, 0))


def before_spec(width, count):
    ratio = CHUNK // 8
    return pl.BlockSpec((8, width), lambda c: (jnp.maximum((count - 1 - c) * ratio - 1, 0), 0))


def sums_spec(flip=None):
    if flip is None:
        return pl.BlockSpec((1, 8, CHUNK), lambda c: (c, 0, 0))
    return pl.BlockSpec((1, 8, CHUNK), lambda c: (flip - 1 - c, 0, 0))


def whole_spec(shape):
    return pl.BlockSpec(shape, lambda c: (0,) * len(shape))


SCALARS = pl.BlockSpec(memory_space=pltpu.SMEM)


def call(kernel, name, chunks, in_specs, outs, scratch, flops, nbytes):
    return pl.pallas_call(
        kernel,
        name=name,
        grid=(chunks,),
        in_specs=in_specs,
        out_specs=[spec for spec, _, _ in outs],
        out_shape=[jax.ShapeDtypeStruct(shape, kind) for _, shape, kind in outs],
        scratch_shapes=scratch,
        compiler_params=pltpu.CompilerParams(
            dimension_semantics=("arbitrary",), vmem_limit_bytes=VMEM_LIMIT
        ),
        cost_estimate=pl.CostEstimate(flops=flops, bytes_accessed=nbytes, transcendentals=0),
    )


def swap(value, distance):
    count = lax.axis_size("head")
    return lax.ppermute(value, "head", [(i, i ^ distance) for i in range(count)])


def shift(value, axis, distance):
    count = lax.axis_size(axis)
    return lax.ppermute(value, axis, [(i, (i + distance) % count) for i in range(count)])


def pick(stack, position):
    return lax.dynamic_index_in_dim(stack, position, 0, keepdims=False)


def gather_small(value, me):
    stack = jnp.stack([value] + [swap(value, k) for k in range(1, 4)])
    return [pick(stack, jnp.bitwise_xor(me, j)) for j in range(4)]


def to_sequences(value, z):
    shards = lax.axis_size("seq")
    each = value.shape[0] // shards
    local = value.shape[1]
    result = []
    for s in range(each):
        pieces = [pick(value, z * each + s)]
        for k in range(1, shards):
            pieces.append(shift(pick(value, lax.rem(z + k, shards) * each + s), "seq", k))
        ordered = jnp.concatenate(pieces[::-1] * 2, axis=0)
        start = (shards - 1 - z) * local
        result.append(lax.dynamic_slice_in_dim(ordered, start, shards * local, 0))
    return result


def to_tokens(sequences, z):
    shards = lax.axis_size("seq")
    local = sequences[0].shape[0] // shards
    result = []
    for value in sequences:
        parts = value.reshape(shards, local, value.shape[1])
        pieces = [pick(parts, z)]
        for k in range(1, shards):
            pieces.append(shift(pick(parts, lax.rem(z + k, shards)), "seq", k))
        ordered = jnp.stack(pieces[::-1] * 2)
        result.append(lax.dynamic_slice_in_dim(ordered, shards - 1 - z, shards, 0))
    joined = jnp.stack(result, axis=1)
    return joined.reshape(shards * len(sequences), local, joined.shape[-1])


def gather_features(own):
    half = own.shape[0] // 2
    by_x, by_y = swap(own, 1), swap(own, 2)
    far = jnp.concatenate([swap(by_x[:half], 2), swap(by_y[half:], 1)], axis=0)
    return [own, by_x, by_y, far]


def line_sum(value, parts):
    if lax.axis_size("seq") != 4:
        return lax.psum(value, "seq")
    z = lax.axis_index("seq")
    inside = (z == 1) | (z == 2)
    size = value.shape[0] // parts
    result = []
    for i in range(parts):
        piece = value[i * size : (i + 1) * size]
        joined = piece + lax.ppermute(piece, "seq", [(0, 1), (3, 2)])
        joined = joined + lax.ppermute(joined, "seq", [(1, 2), (2, 1)])
        result.append(jnp.where(inside, joined, lax.ppermute(joined, "seq", [(1, 0), (2, 3)])))
    return jnp.concatenate(result, axis=0)


def core_sum(value, parts):
    if lax.axis_size("dp") != 2:
        return line_sum(lax.psum(value, "dp"), parts)
    core = lax.axis_index("dp")
    half = value.shape[0] // 2
    keep = lax.dynamic_slice_in_dim(value, core * half, half, 0)
    give = lax.dynamic_slice_in_dim(value, (1 - core) * half, half, 0)
    mine = line_sum(keep + shift(give, "dp", 1), parts)
    other = shift(mine, "dp", 1)
    ordered = jnp.concatenate([other, mine, other], axis=0)
    return lax.dynamic_slice_in_dim(ordered, (1 - core) * half, 2 * half, 0)


def on_device(
    hidden_in, norm_gain, w_z, w_x, w_bc, w_dt, conv_x, conv_x_bias, conv_bc, conv_bc_bias,
    dt_bias, a_log, skip, gate_gain, w_out, out_grad,
):
    shards = lax.axis_size("seq")
    z, me = lax.axis_index("seq"), lax.axis_index("head")
    length = hidden_in.shape[1] * shards
    part_width = hidden_in.shape[2]
    full_width = w_z.shape[0]
    inner = w_x.shape[1]
    heads = dt_bias.shape[0]
    bc_here = w_bc.shape[1]
    each = hidden_in.shape[0] // shards
    chunks = length // CHUNK
    conv_width = inner + 2 * STATE
    tail_width = conv_width + LANES
    index = jnp.bitwise_xor(me, jnp.arange(4, dtype=jnp.int32))

    tokens = [gather_features(part) for part in to_sequences(hidden_in, z)]

    packed = jnp.concatenate([w_bc, norm_gain.reshape(-1, bc_here)], axis=0)
    packed = gather_small(packed, me)
    w_bc_all = jnp.concatenate([part[:full_width] for part in packed], axis=1)
    gain_all = jnp.stack([part[full_width:].reshape(-1) for part in packed]).astype(F32)
    gain_here = jnp.stack([pick(gain_all, index[k]) for k in range(4)])
    taps_bc_own = jnp.concatenate([conv_bc, conv_bc_bias[None], jnp.zeros((3, bc_here), F32)])
    taps_bc = jnp.concatenate(gather_small(taps_bc_own, me), axis=1)
    taps_x = jnp.concatenate([conv_x, conv_x_bias[None], jnp.zeros((3, inner), F32)])
    taps = jnp.concatenate([taps_x, taps_bc], axis=1)
    w_dt_wide = jnp.pad(w_dt, ((0, 0), (0, LANES - heads)))
    w_all = jnp.concatenate([w_z, w_x, w_bc_all, w_dt_wide], axis=1)
    w_back = jnp.concatenate([w_z, w_x, w_dt_wide], axis=1).T
    w_bc_back = w_bc.T
    w_out_back = w_out.T
    dt_params = jnp.pad(jnp.stack([dt_bias, a_log]), ((0, 6), (0, LANES - heads)))
    skip_wide = jnp.repeat(skip, HEAD_DIM)[None]
    gate_wide = gate_gain[None]
    owner = jnp.arange(inner) // HEAD_DIM
    spread = (jnp.arange(LANES)[:, None] == owner[None, :]).astype(BF)
    collect = (owner[:, None] == jnp.arange(LANES)[None, :]).astype(BF)
    order = jnp.arange(CHUNK)
    lower = (order[:, None] >= order[None, :]).astype(BF)
    upper = (order[:, None] <= order[None, :]).astype(BF)

    x_specs = [rows_spec(part_width)] * 4
    x_flipped = [rows_spec(part_width, chunks)] * 4
    gain_spec = whole_spec((4, part_width))
    rows_inner = rows_spec(inner)

    forward = call(
        forward_kernel,
        "forward_scan",
        chunks,
        [SCALARS] + x_specs + [
            whole_spec(w_all.shape), gain_spec, whole_spec(taps.shape), whole_spec((8, LANES)),
            whole_spec((1, inner)), whole_spec(spread.shape), whole_spec(lower.shape),
        ],
        [
            (rows_inner, (length, inner), F32),
            (rows_spec(tail_width), (length, tail_width), F32),
            (rows_inner, (length, inner), F32),
            (pl.BlockSpec((None, inner, STATE), lambda c: (c, 0, 0)), (chunks, inner, STATE), F32),
        ],
        [pltpu.VMEM((CHUNK + 8, conv_width), F32), pltpu.VMEM((inner, STATE), F32)],
        8 * 10**9, 2 * 10**7,
    )
    ahead = [
        forward(index, *x, w_all, gain_here, taps, dt_params, skip_wide, spread, lower)
        for x in tokens
    ]
    cotangents = [gather_features(part) for part in to_sequences(out_grad, z)]

    score = call(
        score_kernel,
        "gate_sums",
        chunks,
        [SCALARS] + x_specs + [
            whole_spec(w_out_back.shape), rows_inner, rows_inner, whole_spec((1, inner)),
        ],
        [(rows_inner, (length, inner), F32), (sums_spec(), (chunks, 8, CHUNK), F32)],
        [],
        2 * 10**9, 10**7,
    )
    scored = []
    for (gate, _, ssd, _), g in zip(ahead, cotangents):
        d_scaled, sums = score(index, *g, w_out_back, ssd, gate, gate_wide)
        scored.append((d_scaled, [sums] + [swap(sums, k) for k in range(1, 4)]))

    flipped = rows_spec(inner, chunks)
    backward = call(
        functools.partial(backward_kernel, inner * lax.axis_size("head")),
        "backward_scan",
        chunks,
        [SCALARS] + [sums_spec(chunks)] * 4 + [
            flipped, flipped, flipped, rows_spec(tail_width, chunks),
            before_spec(tail_width, chunks),
            pl.BlockSpec((None, inner, STATE), lambda c: (chunks - 1 - c, 0, 0)),
            whole_spec((1, inner)), whole_spec(taps.shape), whole_spec((8, LANES)),
            whole_spec((1, inner)), whole_spec(spread.shape), whole_spec(collect.shape),
            whole_spec(lower.shape), whole_spec(upper.shape),
        ],
        [
            (flipped, (length, inner), BF),
            (flipped, (length, inner), BF),
            (flipped, (length, inner), BF),
            (rows_spec(LANES, chunks), (length, LANES), BF),
            (rows_spec(2 * STATE, chunks), (length, 2 * STATE), F32),
            (whole_spec((8, inner)), (8, inner), F32),
            (whole_spec((8, LANES)), (8, LANES), F32),
        ],
        [
            pltpu.VMEM((CHUNK + 8, conv_width), F32),
            pltpu.VMEM((CHUNK + 8, inner), F32),
            pltpu.VMEM((inner, STATE), F32),
        ],
        12 * 10**9, 2 * 10**7,
    )
    weigh = call(
        weight_kernel,
        "weight_sums",
        chunks,
        [SCALARS] + x_specs + [
            gain_spec, whole_spec(w_back.shape), rows_inner, rows_inner, rows_spec(LANES),
        ],
        [
            (rows_spec(full_width), (length, full_width), F32),
            (whole_spec((full_width, 2 * inner)), (full_width, 2 * inner), F32),
            (whole_spec((full_width, LANES)), (full_width, LANES), F32),
        ],
        [],
        9 * 10**9, 2 * 10**7,
    )
    mix = call(
        mixed_kernel,
        "input_sums",
        chunks,
        [SCALARS] + x_flipped + [gain_spec, whole_spec(w_bc_back.shape)]
        + [rows_spec(bc_here, chunks)] * 5
        + [before_spec(bc_here, chunks), whole_spec((8, bc_here)), rows_spec(full_width, chunks)],
        [
            (rows_spec(part_width, chunks), (length, part_width), F32),
            (rows_spec(part_width, chunks), (length, part_width), BF),
            (rows_spec(part_width, chunks), (length, part_width), BF),
            (rows_spec(part_width, chunks), (length, part_width), BF),
            (sums_spec(chunks), (chunks, 8, CHUNK), F32),
            (whole_spec((full_width, bc_here)), (full_width, bc_here), F32),
            (whole_spec((8, bc_here)), (8, bc_here), F32),
        ],
        [pltpu.VMEM((CHUNK + 8, bc_here), F32), pltpu.VMEM((CHUNK + 8, bc_here), F32)],
        10**9, 2 * 10**7,
    )
    finish = call(
        final_kernel,
        "input_gradient",
        chunks,
        x_specs + [gain_spec] + [rows_spec(part_width)] * 4 + [sums_spec()] * 4
        + [rows_spec(part_width)],
        [
            (rows_spec(part_width), (length, part_width), F32),
            (whole_spec((8, part_width)), (8, part_width), F32),
        ],
        [],
        10**8, 10**7,
    )

    largest = jnp.max(jnp.abs(w_out.astype(F32)))
    largest = functools.reduce(jnp.maximum, gather_small(largest[None], me))
    out_scale = 16.0 / jnp.maximum(largest[0], 1e-30)
    w_out_parts = [
        lax.dynamic_slice_in_dim(w_out, index[k] * part_width, part_width, 1) for k in range(4)
    ]

    totals = None
    block_parts, grad_parts = [], []
    for s in range(each):
        x, g = tokens[s], cotangents[s]
        gate, conv, ssd, states = ahead[s]
        d_scaled, sums = scored[s]
        scaled, d_gate, d_x, d_dt, d_bc, wide, dt_sums = backward(
            index, *sums, ssd, gate, d_scaled, conv, conv, states, gate_wide, taps, dt_params,
            skip_wide, spread, collect, lower, upper,
        )
        d_bc_parts = [
            lax.dynamic_slice_in_dim(d_bc, index[k] * bc_here, bc_here, 1) for k in range(4)
        ]
        d_bc_parts = [d_bc_parts[0]] + [swap(d_bc_parts[k], k) for k in range(1, 4)]

        out_parts = [jnp.dot(scaled, part, preferred_element_type=F32) for part in w_out_parts]
        received = [
            swap((out_parts[k] * out_scale).astype(jnp.float16), k) for k in range(1, 4)
        ]
        block = x[0].astype(F32) + out_parts[0]
        block = block + sum(part.astype(F32) for part in received) / out_scale
        block_parts.append(block.astype(BF))
        g_w_out = jnp.stack(
            [
                lax.dot_general(scaled, part, (((0,), (0,)), ((), ())), preferred_element_type=F32)
                for part in g
            ]
        )

        d_normed, g_wide, g_dt = weigh(index, *x, gain_here, w_back, d_gate, d_x, d_dt)
        conv_own = lax.dynamic_slice_in_dim(conv, inner + me * bc_here, bc_here, 1)
        own, send1, send2, send3, dots, g_bc, taps_sums = mix(
            index, *x, gain_here, w_bc_back, *d_bc_parts, conv_own, conv_own, taps_bc_own, d_normed
        )
        dots = [dots] + [swap(dots, k) for k in range(1, 4)]
        grad, gain_sums = finish(
            *x, gain_here, own, swap(send1, 1), swap(send2, 2), swap(send3, 3), *dots, g[0]
        )
        grad_parts.append(grad)
        now = (g_w_out, g_wide, g_dt[:, :heads], g_bc, wide, dt_sums, taps_sums, gain_sums[0:1])
        totals = now if totals is None else jax.tree.map(jnp.add, totals, now)

    g_w_out, g_wide, g_dt, g_bc, wide, dt_sums, taps_sums, gain_sums = totals
    g_w_out = core_sum(g_w_out.reshape(4 * inner, part_width), 2).reshape(4, inner, part_width)
    g_wide = core_sum(g_wide, 4)
    g_rest = core_sum(jnp.concatenate([g_bc, g_dt], axis=1), 1)
    wide, dt_sums, taps_sums, gain_sums = lax.psum(
        (wide, dt_sums, taps_sums, gain_sums), ("seq", "dp")
    )
    g_w_out = jnp.concatenate([pick(g_w_out, index[j]) for j in range(4)], axis=1)
    return (
        to_tokens(block_parts, z),
        to_tokens(grad_parts, z),
        gain_sums[0],
        g_wide[:, :inner],
        g_wide[:, inner:],
        g_rest[:, :bc_here],
        g_rest[:, bc_here:],
        wide[0:4],
        wide[4],
        taps_sums[0:4],
        taps_sums[4],
        dt_sums[1, :heads],
        dt_sums[0, :heads],
        wide[6].reshape(heads, HEAD_DIM).sum(axis=1),
        wide[5],
        g_w_out,
    )


def fits(mesh, seqs, length):
    shards = mesh.shape["seq"]
    local_seqs = seqs // mesh.shape["dp"]
    return mesh.shape["head"] == 4 and local_seqs % shards == 0 and length % CHUNK == 0


def solution(mesh):
    in_specs = (
        P("dp", "seq", "head"),
        P("head"),
        P(None, "head"),
        P(None, "head"),
        P(None, "head"),
        P(None, "head"),
        P(None, "head"),
        P("head"),
        P(None, "head"),
        P("head"),
        P("head"),
        P("head"),
        P("head"),
        P("head"),
        P("head", None),
        P("dp", "seq", "head"),
    )
    out_specs = (
        P("dp", "seq", "head"),
        P("dp", "seq", "head"),
        P("head"),
        P(None, "head"),
        P(None, "head"),
        P(None, "head"),
        P(None, "head"),
        P(None, "head"),
        P("head"),
        P(None, "head"),
        P("head"),
        P("head"),
        P("head"),
        P("head"),
        P("head"),
        P("head", None),
    )

    def run(*args):
        seqs, length, _ = args[0].shape
        body = on_device if fits(mesh, seqs, length) else on_device_general
        return jax.shard_map(
            body, mesh=mesh, in_specs=in_specs, out_specs=out_specs, check_vma=False
        )(*args)

    return run
```

```python
import functools
import jax
import jax.numpy as jnp
import numpy as np
from jax import lax
from jax.experimental import pallas as pl
from jax.experimental.pallas import tpu as pltpu
from jax.sharding import PartitionSpec as P

HEAD_DIM = 64
STATE = 128


epsilon = 1e-05
highest = lax.Precision.HIGHEST


def from_behind(value, axis, steps):
    count = lax.axis_size(axis)
    leading, last = (max(0, -steps), min(count, count - steps))
    return lax.ppermute(value, axis, [(source, source + steps) for source in range(leading, last)])


def prefix(value, axis, join, neutral, backward):
    count, mine = (lax.axis_size(axis), lax.axis_index(axis))
    pieces = jax.tree.map(lambda part: lax.all_gather(part, axis), value)
    if backward:
        pieces = jax.tree.map(lambda part: part[::-1], pieces)
        mine = count - 1 - mine
    total = jax.tree.map(
        lambda part, zero: jnp.full_like(part, 0) + jnp.asarray(zero, part.dtype), value, neutral
    )

    def turn(position, total):
        longer = join(total, jax.tree.map(lambda part: part[position], pieces))
        return jax.tree.map(lambda new, old: jnp.where(position < mine, new, old), longer, total)

    return lax.fori_loop(0, count - 1, turn, total)


def silu_grad(pre_value):
    gate_sig = jax.nn.sigmoid(pre_value)
    return gate_sig * (1.0 + pre_value * (1.0 - gate_sig))


def chain_step(earlier, later):
    return (earlier[0] + later[0], earlier[1] * jnp.exp(later[0])[:, :, None, None] + later[1])


def on_device_general(
    hidden_in,
    norm_gain,
    w_z,
    w_x,
    w_bc,
    w_dt,
    conv_x,
    conv_x_bias,
    conv_bc,
    conv_bc_bias,
    dt_bias,
    a_log,
    skip,
    gate_gain,
    w_out,
    out_grad,
):
    seq_count, local_len, part_width = hidden_in.shape
    heads_here = dt_bias.shape[0]
    inner_here = w_x.shape[1]
    bc_here = w_bc.shape[1]
    kernel_span = conv_x.shape[0]
    edge_len = kernel_span - 1
    row_count = seq_count * local_len
    whole_x, whole_cot, whole_gain = (
        lax.all_gather(hidden_in, "head", axis=2, tiled=True),
        lax.all_gather(out_grad, "head", axis=2, tiled=True),
        lax.all_gather(norm_gain, "head", axis=0, tiled=True),
    )
    full_width = whole_x.shape[2]
    x_full = whole_x.astype(jnp.float32)
    inv_rms = lax.rsqrt(jnp.mean(x_full * x_full, axis=-1, keepdims=True) + epsilon)
    normed = (
        (x_full * inv_rms * whole_gain.astype(jnp.float32))
        .astype(jnp.bfloat16)
        .reshape(row_count, full_width)
    )
    w_cat = jnp.concatenate([w_z, w_x, w_bc, w_dt], axis=1)
    projected = jnp.dot(normed, w_cat, preferred_element_type=jnp.float32).reshape(
        seq_count, local_len, -1
    )
    conv_end = 2 * inner_here + bc_here
    gate_pre = projected[:, :, :inner_here]
    conv_in = projected[:, :, inner_here:conv_end]
    dt_raw = projected[:, :, conv_end:]
    edge_in = from_behind(conv_in[:, local_len - edge_len :, :], "seq", 1)
    extended = jnp.concatenate([edge_in, conv_in], axis=1)
    kernel = jnp.concatenate([conv_x, conv_bc], axis=1)
    kernel_bias = jnp.concatenate([conv_x_bias, conv_bc_bias], axis=0)
    pre_act = jnp.broadcast_to(kernel_bias, conv_in.shape)
    for tap_index in range(kernel_span):
        pre_act = pre_act + kernel[tap_index] * extended[:, tap_index : tap_index + local_len]
    activated = jax.nn.silu(pre_act)
    x_conv = activated[:, :, :inner_here].astype(jnp.bfloat16)
    bc_all = lax.all_gather(
        activated[:, :, inner_here:].astype(jnp.bfloat16), "head", axis=2, tiled=True
    )
    b_rows = bc_all[:, :, :STATE].astype(jnp.float32)
    c_rows = bc_all[:, :, STATE:].astype(jnp.float32)
    values = x_conv.astype(jnp.float32).reshape(seq_count, local_len, heads_here, HEAD_DIM)
    step_size = jax.nn.softplus(dt_raw + dt_bias)
    decay_rate = -jnp.exp(a_log)
    step_log = step_size * decay_rate
    cumulative = jnp.cumsum(step_log, axis=1)
    total_log = cumulative[:, -1, :]
    cum_heads = cumulative.transpose(0, 2, 1)
    step_heads = step_size.transpose(0, 2, 1)
    causal = jnp.arange(local_len)[:, None] >= jnp.arange(local_len)[None, :]
    gap_log = cum_heads[:, :, :, None] - cum_heads[:, :, None, :]
    decay_mat = jnp.where(causal, jnp.exp(jnp.where(causal, gap_log, 0.0)), 0.0)
    scores = jnp.einsum("btn,bsn->bts", c_rows, b_rows, precision=highest)
    decayed = scores[:, None, :, :] * decay_mat
    weights = decayed * step_heads[:, :, None, :]
    local_out = jnp.einsum("bhts,bshp->bthp", weights, values, precision=highest)
    carry_scale = jnp.exp(total_log[:, None, :] - cumulative)
    carry_weight = carry_scale * step_size
    weighted_values = values * carry_weight[..., None]
    local_state = jnp.einsum("bshp,bsn->bhpn", weighted_values, b_rows, precision=highest)
    empty = (jnp.zeros_like(total_log), jnp.zeros_like(local_state))
    _, state_in = prefix((total_log, local_state), "seq", chain_step, empty, False)
    cum_exp = jnp.exp(cumulative)
    cross_out = cum_exp[..., None] * jnp.einsum(
        "btn,bhpn->bthp", c_rows, state_in, precision=highest
    )
    ssd_out = (local_out + cross_out + skip[:, None] * values).reshape(
        seq_count, local_len, inner_here
    )
    gate_act = jax.nn.silu(gate_pre)
    gated_out = ssd_out * gate_act
    inner_width = inner_here * lax.axis_size("head")
    square_sum = lax.psum(jnp.sum(gated_out * gated_out, axis=-1), "head")
    gate_rms = lax.rsqrt(square_sum / inner_width + epsilon)[..., None]
    scaled = (gated_out * gate_rms * gate_gain).astype(jnp.bfloat16).reshape(row_count, inner_here)
    out_own = lax.psum_scatter(
        lax.dot_general(
            w_out, scaled, (((0,), (1,)), ((), ())), preferred_element_type=jnp.float32
        ),
        "head",
        scatter_dimension=0,
        tiled=True,
    )
    x_own = hidden_in.astype(jnp.float32)
    block_out = (x_own + out_own.T.reshape(seq_count, local_len, part_width)).astype(jnp.bfloat16)
    cot_rows = whole_cot.reshape(row_count, full_width)
    g_w_out = lax.dot_general(
        scaled, cot_rows, (((0,), (0,)), ((), ())), preferred_element_type=jnp.float32
    )
    d_scaled = lax.dot_general(
        cot_rows, w_out, (((1,), (1,)), ((), ())), preferred_element_type=jnp.float32
    )
    d_scaled = d_scaled.reshape(seq_count, local_len, inner_here)
    g_gate_gain = jnp.sum(d_scaled * gated_out * gate_rms, axis=(0, 1))
    gain_term = d_scaled * gate_gain
    inner_dot = lax.psum(jnp.sum(gain_term * gated_out, axis=-1), "head")
    d_gated = gate_rms * gain_term - gated_out * gate_rms**3 * (inner_dot / inner_width)[..., None]
    d_gate = d_gated * ssd_out * silu_grad(gate_pre)
    d_out = (d_gated * gate_act).reshape(seq_count, local_len, heads_here, HEAD_DIM)
    g_skip = jnp.sum(d_out * values, axis=(0, 1, 3))
    gram = jnp.einsum("bthp,bshp->bhts", d_out, values, precision=highest)
    d_values = (
        jnp.einsum("bhts,bthp->bshp", weights, d_out, precision=highest) + skip[:, None] * d_out
    )
    masked = gram * decayed
    d_scores = jnp.sum(gram * decay_mat * step_heads[:, :, None, :], axis=1)
    d_step_intra = jnp.sum(masked, axis=2).transpose(0, 2, 1)
    d_gap = masked * step_heads[:, :, None, :]
    d_cum_intra = (jnp.sum(d_gap, axis=3) - jnp.sum(d_gap, axis=2)).transpose(0, 2, 1)
    d_c = jnp.einsum("bts,bsn->btn", d_scores, b_rows, precision=highest)
    d_b = jnp.einsum("bts,btn->bsn", d_scores, c_rows, precision=highest)
    d_out_exp = d_out * cum_exp[..., None]
    d_c = d_c + jnp.einsum("bthp,bhpn->btn", d_out_exp, state_in, precision=highest)
    d_state_in = jnp.einsum("bthp,btn->bhpn", d_out_exp, c_rows, precision=highest)
    d_cum_cross = jnp.sum(d_out * cross_out, axis=3)
    _, d_local_state = prefix((total_log, d_state_in), "seq", chain_step, empty, True)
    state_back = jnp.einsum("bhpn,bsn->bshp", d_local_state, b_rows, precision=highest)
    d_values = d_values + carry_weight[..., None] * state_back
    d_b = d_b + jnp.einsum("bshp,bhpn->bsn", weighted_values, d_local_state, precision=highest)
    d_carry = jnp.sum(values * state_back, axis=3)
    carry_prod = d_carry * carry_weight
    d_total = jnp.exp(total_log) * jnp.sum(state_in * d_local_state, axis=(2, 3)) + jnp.sum(
        carry_prod, axis=1
    )
    d_cum = d_cum_intra + d_cum_cross - carry_prod
    d_cum = d_cum.at[:, -1, :].add(d_total)
    d_step_log = jnp.cumsum(d_cum[:, ::-1, :], axis=1)[:, ::-1, :]
    d_step = d_step_intra + d_carry * carry_scale + d_step_log * decay_rate
    g_a_log = jnp.sum(d_step_log * step_log, axis=(0, 1))
    d_dt_pre = d_step * jax.nn.sigmoid(dt_raw + dt_bias)
    g_dt_bias = jnp.sum(d_dt_pre, axis=(0, 1))
    d_bc_own = lax.psum_scatter(
        jnp.concatenate([d_b, d_c], axis=2), "head", scatter_dimension=2, tiled=True
    )
    d_act = jnp.concatenate([d_values.reshape(seq_count, local_len, inner_here), d_bc_own], axis=2)
    d_pre = d_act * silu_grad(pre_act)
    g_kernel = jnp.stack(
        [
            jnp.sum(d_pre * extended[:, tap_index : tap_index + local_len], axis=(0, 1))
            for tap_index in range(kernel_span)
        ]
    )
    g_kernel_bias = jnp.sum(d_pre, axis=(0, 1))
    d_padded = jnp.pad(d_pre, ((0, 0), (edge_len, edge_len), (0, 0)))
    d_ext = jnp.zeros_like(extended)
    for tap_index in range(kernel_span):
        offset = edge_len - tap_index
        d_ext = d_ext + kernel[tap_index] * d_padded[:, offset : offset + local_len + edge_len]
    back_edge = from_behind(d_ext[:, :edge_len, :], "seq", -1)
    d_conv_in = d_ext[:, edge_len:, :].at[:, local_len - edge_len :, :].add(back_edge)
    d_proj = (
        jnp.concatenate([d_gate, d_conv_in, d_dt_pre], axis=2)
        .astype(jnp.bfloat16)
        .reshape(row_count, -1)
    )
    g_w_cat = lax.dot_general(
        normed, d_proj, (((0,), (0,)), ((), ())), preferred_element_type=jnp.float32
    )
    x_hat_own = x_own * inv_rms
    gain_own = norm_gain.astype(jnp.float32)
    d_own = lax.psum_scatter(
        lax.dot_general(
            w_cat, d_proj, (((1,), (1,)), ((), ())), preferred_element_type=jnp.float32
        ),
        "head",
        scatter_dimension=0,
        tiled=True,
    ).T.reshape(seq_count, local_len, part_width)
    d_hat_own = d_own * gain_own
    row_mean = lax.psum(jnp.sum(d_hat_own * x_hat_own, axis=-1), "head")[..., None] / full_width
    grad_in = out_grad.astype(jnp.float32) + inv_rms * (d_hat_own - x_hat_own * row_mean)
    g_norm_gain = jnp.sum(d_own * x_hat_own, axis=(0, 1))
    (
        g_norm_gain,
        g_w_cat,
        g_kernel,
        g_kernel_bias,
        g_dt_bias,
        g_a_log,
        g_skip,
        g_gate_gain,
        g_w_out,
    ) = lax.psum(
        (
            g_norm_gain,
            g_w_cat,
            g_kernel,
            g_kernel_bias,
            g_dt_bias,
            g_a_log,
            g_skip,
            g_gate_gain,
            g_w_out,
        ),
        ("seq", "dp"),
    )
    g_w_z = g_w_cat[:, :inner_here]
    g_w_x = g_w_cat[:, inner_here : 2 * inner_here]
    g_w_bc = g_w_cat[:, 2 * inner_here : conv_end]
    g_w_dt = g_w_cat[:, conv_end:]
    return (
        block_out,
        grad_in,
        g_norm_gain,
        g_w_z,
        g_w_x,
        g_w_bc,
        g_w_dt,
        g_kernel[:, :inner_here],
        g_kernel_bias[:inner_here],
        g_kernel[:, inner_here:],
        g_kernel_bias[inner_here:],
        g_dt_bias,
        g_a_log,
        g_skip,
        g_gate_gain,
        g_w_out,
    )


BF = jnp.bfloat16
F32 = jnp.float32
CHUNK = 256
LANES = 128
VMEM_LIMIT = 56 * 1024 * 1024


def dot_nn(a, b):
    return lax.dot_general(a, b, (((1,), (0,)), ((), ())), preferred_element_type=F32)


def dot_nt(a, b):
    return lax.dot_general(a, b, (((1,), (1,)), ((), ())), preferred_element_type=F32)


def dot_tn(a, b):
    return lax.dot_general(a, b, (((0,), (0,)), ((), ())), preferred_element_type=F32)


def split2(value):
    high = value.astype(BF)
    return high, (value - high.astype(F32)).astype(BF)


def split3(value):
    high = value.astype(BF)
    rest = value - high.astype(F32)
    middle = rest.astype(BF)
    return high, middle, (rest - middle.astype(F32)).astype(BF)


def sigmoid(value):
    return 1.0 / (1.0 + jnp.exp(-value))


def silu_slope(value, sig):
    return sig * (1.0 + value * (1.0 - sig))


def step_values(dt_block, dt_params):
    shifted = dt_block + dt_params[0:1]
    step = jnp.maximum(shifted, 0.0) + jnp.log1p(jnp.exp(-jnp.abs(shifted)))
    rate = -jnp.exp(dt_params[1:2])
    return shifted, step, rate, step * rate


def inverse_rms(blocks):
    total = sum(jnp.sum(block * block, axis=1, keepdims=True) for block in blocks)
    return lax.rsqrt(total / (len(blocks) * blocks[0].shape[1]) + epsilon)


def normed_blocks(x_refs, gain_ref):
    blocks = [ref[...].astype(F32) for ref in x_refs]
    inverse = inverse_rms(blocks)
    hats = [block * inverse for block in blocks]
    return inverse, hats, [(hat * gain_ref[k : k + 1]).astype(BF) for k, hat in enumerate(hats)]


def block_of(index_ref, k, size):
    return pl.ds(pl.multiple_of(index_ref[k] * size, size), size)


def column_of_sums(rows, lanes_here):
    tile = jnp.zeros((CHUNK, LANES), F32)
    lane = lax.broadcasted_iota(jnp.int32, (CHUNK, LANES), 1)
    for position, value in enumerate(rows):
        tile = jnp.where(lane == position, value, tile)
    return jnp.transpose(tile)[0:lanes_here]


def forward_kernel(
    index_ref, x0, x1, x2, x3, w_z_ref, w_x_ref, w_rest_ref, gain_ref, taps_ref, dt_ref, skip_ref,
    spread_ref, lower_ref, gate_out, conv_out, ssd_out, state_out, extended, state,
):
    inner = skip_ref.shape[1]
    heads = inner // HEAD_DIM
    conv_width = inner + 2 * STATE

    @pl.when(pl.program_id(0) == 0)
    def _():
        extended[0:8, :] = jnp.zeros((8, conv_width), F32)
        state[...] = jnp.zeros(state.shape, F32)

    x_refs = (x0, x1, x2, x3)
    _, _, normed = normed_blocks(x_refs, gain_ref)
    parts = [block_of(index_ref, k, part.shape[1]) for k, part in enumerate(normed)]
    gate_out[...] = sum(dot_nn(part, w_z_ref[rows, :]) for part, rows in zip(normed, parts))
    projected = jnp.concatenate(
        [
            sum(dot_nn(part, ref[rows, :]) for part, rows in zip(normed, parts))
            for ref in (w_x_ref, w_rest_ref)
        ],
        axis=1,
    )
    conv_out[...] = projected
    conv_in = projected[:, :conv_width]
    extended[8 : 8 + CHUNK, :] = conv_in
    pre_act = taps_ref[4:5, :] + taps_ref[3:4, :] * conv_in
    for k in range(3):
        pre_act = pre_act + taps_ref[k : k + 1, :] * extended[5 + k : 5 + k + CHUNK, :]
    extended[0:8, :] = conv_in[CHUNK - 8 :, :]
    act = (pre_act * sigmoid(pre_act)).astype(BF)
    values = act[:, :inner]
    b_rows = act[:, inner : inner + STATE]
    c_rows = act[:, inner + STATE :]

    _, step, _, step_log = step_values(projected[:, conv_width:], dt_ref)
    cumulative = sum(dot_nn(lower_ref[...], part) for part in split3(step_log))
    cum_t = jnp.transpose(cumulative)
    step_t = jnp.transpose(step)
    total = cumulative[CHUNK - 1 : CHUNK, :]
    spread = spread_ref[...]
    widened = jnp.concatenate([jnp.exp(cumulative), jnp.exp(total - cumulative) * step], axis=0)
    high, low = split2(widened)
    widened = dot_nn(high, spread) + dot_nn(low, spread)
    cum_exp, carry_weight = widened[:CHUNK], widened[CHUNK:]

    state_now = state[...]
    state_out[...] = state_now
    s_high, s_low = split2(state_now)
    cross = dot_nt(c_rows, s_high) + dot_nt(c_rows, s_low)
    values_f = values.astype(F32)
    carried = cum_exp * cross + skip_ref[...] * values_f

    scores = dot_nt(c_rows, b_rows)
    row = lax.broadcasted_iota(jnp.int32, (CHUNK, CHUNK), 0)
    column = lax.broadcasted_iota(jnp.int32, (CHUNK, CHUNK), 1)
    causal = row >= column
    lane = lax.broadcasted_iota(jnp.int32, (CHUNK, LANES), 1)
    for pair in range(heads // 2):
        lanes = slice(pair * LANES, (pair + 1) * LANES)
        total_out = carried[:, lanes]
        for side in range(2):
            h = 2 * pair + side
            mine = (lane >= HEAD_DIM) if side else (lane < HEAD_DIM)
            own_values = jnp.where(mine, values[:, lanes], jnp.zeros((), BF))
            gap = cumulative[:, h : h + 1] - cum_t[h : h + 1, :]
            decay = jnp.exp(jnp.where(causal, gap, -1e30))
            high, low = split2(scores * decay * step_t[h : h + 1, :])
            total_out = total_out + dot_nn(high, own_values) + dot_nn(low, own_values)
        ssd_out[:, lanes] = total_out

    high, low = split2(values_f * carry_weight)
    grown = dot_tn(high, b_rows) + dot_tn(low, b_rows)
    total_t = jnp.exp(cum_t[:, CHUNK - 1 : CHUNK])
    for h in range(heads):
        part = slice(h * HEAD_DIM, (h + 1) * HEAD_DIM)
        state[part, :] = total_t[h : h + 1, :] * state_now[part] + grown[part]


def score_kernel(index_ref, g0, g1, g2, g3, w_ref, ssd_ref, gate_ref, gain_ref, d_out, sums_out):
    d_scaled = sum(
        dot_nn(ref[...], w_ref[block_of(index_ref, k, ref.shape[1]), :])
        for k, ref in enumerate((g0, g1, g2, g3))
    )
    d_out[...] = d_scaled
    gate = gate_ref[...]
    gated = ssd_ref[...] * (gate * sigmoid(gate))
    squares = jnp.sum(gated * gated, axis=1, keepdims=True)
    inner_dot = jnp.sum(d_scaled * gain_ref[...] * gated, axis=1, keepdims=True)
    sums_out[0] = column_of_sums((squares, inner_dot), 8)


def backward_kernel(
    inner_width, index_ref, q0, q1, q2, q3, ssd_ref, gate_ref, d_scaled_ref, conv_ref, before_ref,
    state_ref, gain_ref, taps_ref, dt_ref, skip_ref, spread_ref, gather_ref, lower_ref, upper_ref,
    scaled_out, d_gate_out, d_x_out, d_dt_out, d_bc_out, wide_out, dt_out,
    extended, d_pre, state_grad,
):
    inner = skip_ref.shape[1]
    heads = inner // HEAD_DIM
    conv_width = inner + 2 * STATE
    step_at = pl.program_id(0)
    chunk_at = pl.num_programs(0) - 1 - step_at

    @pl.when(step_at == 0)
    def _():
        d_pre[CHUNK : CHUNK + 8, :] = jnp.zeros((8, inner), F32)
        state_grad[...] = jnp.zeros(state_grad.shape, F32)
        wide_out[...] = jnp.zeros(wide_out.shape, F32)
        dt_out[...] = jnp.zeros(dt_out.shape, F32)

    sums = q0[0] + q1[0] + q2[0] + q3[0]
    sums = jnp.transpose(jnp.concatenate([sums, jnp.zeros((LANES - 8, CHUNK), F32)], axis=0))
    rms = lax.rsqrt(sums[:, 0:1] / inner_width + epsilon)
    mean_dot = sums[:, 1:2] / inner_width
    gate = gate_ref[...]
    gate_sig = sigmoid(gate)
    gate_act = gate * gate_sig
    ssd = ssd_ref[...]
    gated = ssd * gate_act
    gated_rms = gated * rms
    gain = gain_ref[...]
    d_scaled = d_scaled_ref[...]
    scaled_out[...] = (gated_rms * gain).astype(BF)
    wide_out[5:6, :] += jnp.sum(d_scaled * gated_rms, axis=0, keepdims=True)
    d_gated = rms * (d_scaled * gain) - gated * (rms * rms * rms * mean_dot)
    d_gate_out[...] = (d_gated * ssd * silu_slope(gate, gate_sig)).astype(BF)
    d_ssd = d_gated * gate_act

    conv_in = conv_ref[:, :conv_width]
    extended[0:8, :] = jnp.where(chunk_at > 0, before_ref[:, :conv_width], 0.0)
    extended[8 : 8 + CHUNK, :] = conv_in
    pre_act = taps_ref[4:5, :] + taps_ref[3:4, :] * conv_in
    for k in range(3):
        pre_act = pre_act + taps_ref[k : k + 1, :] * extended[5 + k : 5 + k + CHUNK, :]
    sig = sigmoid(pre_act)
    act = (pre_act * sig).astype(BF)
    slope_x = silu_slope(pre_act[:, :inner], sig[:, :inner])
    values = act[:, :inner]
    values_f = values.astype(F32)
    b_rows = act[:, inner : inner + STATE]
    c_rows = act[:, inner + STATE :]
    wide_out[6:7, :] += jnp.sum(d_ssd * values_f, axis=0, keepdims=True)

    shifted, step, rate, step_log = step_values(conv_ref[:, conv_width:], dt_ref)
    cumulative = sum(dot_nn(lower_ref[...], part) for part in split3(step_log))
    cum_t = jnp.transpose(cumulative)
    total = cumulative[CHUNK - 1 : CHUNK, :]
    carry_scale = jnp.exp(total - cumulative)
    carry = carry_scale * step
    spread = spread_ref[...]
    high, low = split2(jnp.concatenate([jnp.exp(cumulative), carry], axis=0))
    widened = dot_nn(high, spread) + dot_nn(low, spread)
    cum_exp, carry_weight = widened[:CHUNK], widened[CHUNK:]

    scores = dot_nt(b_rows, c_rows)
    row = lax.broadcasted_iota(jnp.int32, (CHUNK, CHUNK), 0)
    column = lax.broadcasted_iota(jnp.int32, (CHUNK, CHUNK), 1)
    causal = row <= column
    lane = lax.broadcasted_iota(jnp.int32, (CHUNK, LANES), 1)

    s_high, s_low = split2(state_ref[...])
    r_now = state_grad[...]
    r_high, r_low = split2(r_now)
    cross = cum_exp * (dot_nt(c_rows, s_high) + dot_nt(c_rows, s_low))
    back = dot_nt(b_rows, r_high) + dot_nt(b_rows, r_low)
    d_values = carry_weight * back + skip_ref[...] * d_ssd

    d_scores = jnp.zeros((CHUNK, CHUNK), F32)
    step_intra = jnp.zeros((CHUNK, LANES), F32)
    row_sums = []
    d_parts = []
    for pair in range(heads // 2):
        lanes = slice(pair * LANES, (pair + 1) * LANES)
        g_high, g_low = split2(d_ssd[:, lanes])
        part = d_values[:, lanes]
        for side in range(2):
            h = 2 * pair + side
            mine = (lane >= HEAD_DIM) if side else (lane < HEAD_DIM)
            zero = jnp.zeros((), BF)
            own_values = jnp.where(mine, values[:, lanes], zero)
            own_high = jnp.where(mine, g_high, zero)
            own_low = jnp.where(mine, g_low, zero)
            gram = dot_nt(own_values, g_high) + dot_nt(own_values, g_low)
            gap = cum_t[h : h + 1, :] - cumulative[:, h : h + 1]
            decay = jnp.exp(jnp.where(causal, gap, -1e30))
            step_column = step[:, h : h + 1]
            pulled = gram * decay
            masked = pulled * scores
            d_scores = d_scores + pulled * step_column
            step_intra = jnp.where(
                lane == h, jnp.sum(masked, axis=1, keepdims=True), step_intra
            )
            row_sums.append(jnp.sum(masked * step_column, axis=0, keepdims=True))
            w_high, w_low = split2(scores * decay * step_column)
            part = part + dot_nn(w_high, own_high)
            part = part + dot_nn(w_low, own_high)
            part = part + dot_nn(w_high, own_low)
        d_parts.append(part)
    d_values = jnp.concatenate(d_parts, axis=1)

    high, low = split2(d_scores)
    d_b = dot_nn(high, c_rows) + dot_nn(low, c_rows)
    d_c = dot_tn(high, b_rows) + dot_tn(low, b_rows)
    d_ssd_exp = d_ssd * cum_exp
    e_high, e_low = split2(d_ssd_exp)
    d_c = d_c + dot_nn(e_high, s_high) + dot_nn(e_low, s_high) + dot_nn(e_high, s_low)
    weighted = values_f * carry_weight
    v_high, v_low = split2(weighted)
    d_b = d_b + dot_nn(v_high, r_high) + dot_nn(v_low, r_high) + dot_nn(v_high, r_low)
    d_bc_out[...] = jnp.concatenate([d_b, d_c], axis=1)

    gather = gather_ref[...]
    d_cum_cross = sum(dot_nn(p, gather) for p in split3(d_ssd * cross))
    d_carry = sum(dot_nn(p, gather) for p in split3(values_f * back))
    carry_prod = d_carry * carry
    kept = state_ref[...] * r_now
    kept = sum(dot_tn(gather, p) for p in split3(kept))
    kept = jnp.sum(kept, axis=1, keepdims=True)
    kept = jnp.transpose(jnp.broadcast_to(kept, (LANES, LANES)))[0:1]
    d_total = jnp.exp(total) * kept + jnp.sum(carry_prod, axis=0, keepdims=True)
    rows_t = jnp.concatenate(row_sums + [jnp.zeros((LANES - heads, CHUNK), F32)], axis=0)
    d_cum = jnp.transpose(rows_t) - step * step_intra + d_cum_cross - carry_prod
    last = lax.broadcasted_iota(jnp.int32, (CHUNK, LANES), 0) == CHUNK - 1
    d_cum = d_cum + jnp.where(last, d_total, 0.0)
    d_step_log = sum(dot_nn(upper_ref[...], p) for p in split3(d_cum))
    d_step = step_intra + d_carry * carry_scale + d_step_log * rate
    dt_out[0:1, :] += jnp.sum(d_step_log * step_log, axis=0, keepdims=True)
    d_dt = d_step * sigmoid(shifted)
    dt_out[1:2, :] += jnp.sum(d_dt, axis=0, keepdims=True)
    d_dt_out[...] = d_dt.astype(BF)

    grown = dot_tn(e_high, c_rows) + dot_tn(e_low, c_rows)
    total_t = jnp.exp(cum_t[:, CHUNK - 1 : CHUNK])
    for h in range(heads):
        part = slice(h * HEAD_DIM, (h + 1) * HEAD_DIM)
        state_grad[part, :] = total_t[h : h + 1, :] * r_now[part] + grown[part]

    d_pre_now = d_values * slope_x
    d_pre[0:CHUNK, :] = d_pre_now
    wide_out[4:5, :] += jnp.sum(d_pre_now, axis=0, keepdims=True)
    d_in = taps_ref[3:4, :inner] * d_pre_now
    wide_out[3:4, :] += jnp.sum(d_pre_now * conv_in[:, :inner], axis=0, keepdims=True)
    for k in range(3):
        earlier = extended[5 + k : 5 + k + CHUNK, :inner]
        wide_out[k : k + 1, :] += jnp.sum(d_pre_now * earlier, axis=0, keepdims=True)
        d_in = d_in + taps_ref[k : k + 1, :inner] * d_pre[3 - k : 3 - k + CHUNK, :]
    d_x_out[...] = d_in.astype(BF)
    d_pre[CHUNK : CHUNK + 8, :] = d_pre_now[0:8, :]


def weight_kernel(
    index_ref, x0, x1, x2, x3, g0, g1, g2, g3, gain_ref, w_ref, scaled_ref, d_gate_ref, d_x_ref,
    d_dt_ref, *rest,
):
    *sums_so_far, d_normed_out, wide_out, dt_out, out_out = rest

    @pl.when(pl.program_id(0) == 0)
    def _():
        for i, ref in enumerate((wide_out, dt_out, out_out)):
            ref[...] = sums_so_far[i][...] if sums_so_far else jnp.zeros(ref.shape, F32)

    _, _, normed = normed_blocks((x0, x1, x2, x3), gain_ref)
    d_wide = jnp.concatenate([d_gate_ref[...], d_x_ref[...]], axis=1)
    d_dt = d_dt_ref[...]
    d_all = jnp.concatenate([d_wide, d_dt], axis=1)
    scaled = scaled_ref[...]
    width = normed[0].shape[1]
    for k, (part, cot) in enumerate(zip(normed, (g0, g1, g2, g3))):
        rows = block_of(index_ref, k, width)
        wide_out[rows, :] += dot_tn(part, d_wide)
        dt_out[rows, :] += dot_tn(part, d_dt)
        out_out[:, k * width : (k + 1) * width] += dot_tn(scaled, cot[...])
        d_normed_out[:, k * width : (k + 1) * width] = dot_nn(d_all, w_ref[:, rows])


def mixed_kernel(
    index_ref, x0, x1, x2, x3, gain_ref, w_ref, d_act_ref, conv_ref, before_ref, taps_ref,
    d_normed_ref, own_out, send1, send2, send3, grad_out, taps_out, extended, d_pre,
):
    step_at = pl.program_id(0)
    chunk_at = pl.num_programs(0) - 1 - step_at
    own = conv_ref.shape[1]

    @pl.when(step_at == 0)
    def _():
        d_pre[CHUNK : CHUNK + 8, :] = jnp.zeros((8, own), F32)
        grad_out[...] = jnp.zeros(grad_out.shape, F32)
        taps_out[...] = jnp.zeros(taps_out.shape, F32)

    conv_in = conv_ref[...]
    extended[0:8, :] = jnp.where(chunk_at > 0, before_ref[...], 0.0)
    extended[8 : 8 + CHUNK, :] = conv_in
    pre_act = taps_ref[4:5, :] + taps_ref[3:4, :] * conv_in
    for k in range(3):
        pre_act = pre_act + taps_ref[k : k + 1, :] * extended[5 + k : 5 + k + CHUNK, :]
    d_pre_now = d_act_ref[...] * silu_slope(pre_act, sigmoid(pre_act))
    d_pre[0:CHUNK, :] = d_pre_now
    taps_out[4:5, :] += jnp.sum(d_pre_now, axis=0, keepdims=True)
    taps_out[3:4, :] += jnp.sum(d_pre_now * conv_in, axis=0, keepdims=True)
    d_in = taps_ref[3:4, :] * d_pre_now
    for k in range(3):
        earlier = extended[5 + k : 5 + k + CHUNK, :]
        taps_out[k : k + 1, :] += jnp.sum(d_pre_now * earlier, axis=0, keepdims=True)
        d_in = d_in + taps_ref[k : k + 1, :] * d_pre[3 - k : 3 - k + CHUNK, :]
    d_pre[CHUNK : CHUNK + 8, :] = d_pre_now[0:8, :]
    d_in = d_in.astype(BF)

    _, hats, normed = normed_blocks((x0, x1, x2, x3), gain_ref)
    width = normed[0].shape[1]
    row_dot = jnp.zeros((CHUNK, 1), F32)
    sends = (own_out, send1, send2, send3)
    for k, out in enumerate(sends):
        rows = block_of(index_ref, k, width)
        grad_out[rows, :] += dot_tn(normed[k], d_in)
        d_part = d_normed_ref[:, k * width : (k + 1) * width] + dot_nn(d_in, w_ref[:, rows])
        out[0, 0:CHUNK, :] = d_part.astype(out.dtype)
        scaled_hat = hats[k] * gain_ref[k : k + 1]
        row_dot = row_dot + jnp.sum(d_part * scaled_hat, axis=1, keepdims=True)
    dots = column_of_sums((row_dot,), 8)
    own_out[0, CHUNK : CHUNK + 8, :] = dots
    high, low = split2(dots)
    first = lax.broadcasted_iota(jnp.int32, (8, CHUNK), 0) == 0
    low = jnp.where(first, low.astype(F32), 0.0)
    low = jnp.concatenate([low[0:1], low[0:1], jnp.zeros((6, CHUNK), F32)], axis=0)
    high = high.astype(F32)
    both = jnp.where(first, high, low)
    both = jnp.concatenate([both, jnp.zeros((8, CHUNK), F32)], axis=0).astype(BF)
    for out in sends[1:]:
        out[0, CHUNK : CHUNK + 16, :] = both


def final_kernel(x0, x1, x2, x3, gain_ref, own_ref, r1, r2, r3, cot_ref, grad_out, gain_out):
    @pl.when(pl.program_id(0) == 0)
    def _():
        gain_out[...] = jnp.zeros(gain_out.shape, F32)

    blocks = [ref[...].astype(F32) for ref in (x0, x1, x2, x3)]
    inverse = inverse_rms(blocks)
    hat = blocks[0] * inverse
    received = [ref[0].astype(F32) for ref in (r1, r2, r3)]
    total = received[0] + received[1] + received[2]
    sums = own_ref[0, CHUNK : CHUNK + 8, :] + total[CHUNK : CHUNK + 8, :]
    sums = jnp.transpose(jnp.concatenate([sums, jnp.zeros((LANES - 8, CHUNK), F32)], axis=0))
    mean = (sums[:, 0:1] + sums[:, 1:2]) / (len(blocks) * hat.shape[1])
    d_own = own_ref[0, 0:CHUNK, :] + total[0:CHUNK]
    gain_out[0:1, :] += jnp.sum(d_own * hat, axis=0, keepdims=True)
    d_hat = d_own * gain_ref[0:1]
    grad = cot_ref[...].astype(F32) + inverse * (d_hat - hat * mean)
    grad_out[...] = grad
    top = jnp.max(jnp.abs(grad), axis=0, keepdims=True)
    gain_out[1:2, :] = jnp.maximum(gain_out[1:2, :], top)


def rows_spec(width, flip=None):
    if flip is None:
        return pl.BlockSpec((CHUNK, width), lambda c: (c, 0))
    return pl.BlockSpec((CHUNK, width), lambda c: (flip - 1 - c, 0))


def before_spec(width, count):
    ratio = CHUNK // 8
    return pl.BlockSpec((8, width), lambda c: (jnp.maximum((count - 1 - c) * ratio - 1, 0), 0))


def sums_spec(flip=None):
    if flip is None:
        return pl.BlockSpec((1, 8, CHUNK), lambda c: (c, 0, 0))
    return pl.BlockSpec((1, 8, CHUNK), lambda c: (flip - 1 - c, 0, 0))


def part_spec(more, width, flip=None):
    if flip is None:
        return pl.BlockSpec((1, CHUNK + more, width), lambda c: (c, 0, 0))
    return pl.BlockSpec((1, CHUNK + more, width), lambda c: (flip - 1 - c, 0, 0))


def whole_spec(shape):
    return pl.BlockSpec(shape, lambda c: (0,) * len(shape))


SCALARS = pl.BlockSpec(memory_space=pltpu.SMEM)


def call(kernel, name, chunks, in_specs, outs, scratch, flops, nbytes):
    return pl.pallas_call(
        kernel,
        name=name,
        grid=(chunks,),
        in_specs=in_specs,
        out_specs=[spec for spec, _, _ in outs],
        out_shape=[jax.ShapeDtypeStruct(shape, kind) for _, shape, kind in outs],
        scratch_shapes=scratch,
        compiler_params=pltpu.CompilerParams(
            dimension_semantics=("arbitrary",), vmem_limit_bytes=VMEM_LIMIT
        ),
        cost_estimate=pl.CostEstimate(flops=flops, bytes_accessed=nbytes, transcendentals=0),
    )


def swap(value, distance):
    count = lax.axis_size("head")
    return lax.ppermute(value, "head", [(i, i ^ distance) for i in range(count)])


def shift(value, axis, distance):
    count = lax.axis_size(axis)
    return lax.ppermute(value, axis, [(i, (i + distance) % count) for i in range(count)])


def pick(stack, position):
    return lax.dynamic_index_in_dim(stack, position, 0, keepdims=False)


def after(value, *earlier):
    return lax.optimization_barrier((value, earlier))[0]


def exchange(parts, z):
    shards = lax.axis_size("seq")
    pieces = [pick(parts, z)]
    for k in range(1, shards):
        pieces.append(shift(pick(parts, lax.rem(z + k, shards)), "seq", k))
    return pieces


def in_order(pieces, z, axis):
    size = pieces[0].shape[axis]
    count = len(pieces)
    ordered = jnp.concatenate(pieces[::-1] * 2, axis=axis)
    return lax.dynamic_slice_in_dim(ordered, (count - 1 - z) * size, count * size, axis)


def to_sequences(value, z):
    shards = lax.axis_size("seq")
    parts = value.reshape((shards, -1) + value.shape[1:])
    return in_order(exchange(parts, z), z, 1)


def to_tokens(value, z, top=None):
    shards = lax.axis_size("seq")
    parts = value.reshape(shards, value.shape[0] // shards, value.shape[1])
    if top is None:
        return in_order([piece[None] for piece in exchange(parts, z)], z, 0)
    power = exponent_of(top)
    pieces = [pick(parts, z)]
    for k in range(1, shards):
        payload = to_half(pick(parts, lax.rem(z + k, shards)), power)
        pieces.append(from_half(shift(payload, "seq", k))[0])
    return in_order([piece[None] for piece in pieces], z, 0)


def joined_tokens(parts):
    joined = jnp.stack(parts, axis=1)
    return joined.reshape((-1,) + joined.shape[2:])


def far_features(by_x, by_y):
    half = by_x.shape[0] // 2
    return jnp.concatenate([swap(by_x[:half], 2), swap(by_y[half:], 1)], axis=0)


HALF_TOP = 8.0


def exponent_of(top):
    return jnp.ceil(jnp.log2(jnp.maximum(top, 1e-30)))


def to_half(value, exponent):
    body = (value * jnp.exp2(HALF_TOP - exponent)).astype(jnp.float16)
    mark = jnp.full((16, value.shape[1]), exponent, F32).astype(jnp.float16)
    return jnp.concatenate([body, mark], axis=0)


def from_half(payload):
    exponent = payload[-1, 0].astype(F32)
    return payload[:-16].astype(F32) * jnp.exp2(exponent - HALF_TOP), exponent


def butterfly_sum(value):
    for axis in ("dp", "seq"):
        distance = 1
        while distance < lax.axis_size(axis):
            pairs = [(i, i ^ distance) for i in range(lax.axis_size(axis))]
            value = value + lax.ppermute(value, axis, pairs)
            distance *= 2
    return value


def on_device(
    hidden_in, norm_gain, w_z, w_x, w_bc, w_dt, conv_x, conv_x_bias, conv_bc, conv_bc_bias,
    dt_bias, a_log, skip, gate_gain, w_out, out_grad,
):
    shards = lax.axis_size("seq")
    z, me = lax.axis_index("seq"), lax.axis_index("head")
    length = hidden_in.shape[1] * shards
    part_width = hidden_in.shape[2]
    full_width = w_z.shape[0]
    inner = w_x.shape[1]
    heads = dt_bias.shape[0]
    bc_here = w_bc.shape[1]
    each = hidden_in.shape[0] // shards
    chunks = length // CHUNK
    conv_width = inner + 2 * STATE
    tail_width = conv_width + LANES
    index = jnp.bitwise_xor(me, jnp.arange(4, dtype=jnp.int32))

    hidden = to_sequences(hidden_in, z)

    largest = jnp.max(jnp.abs(w_out.astype(F32)))
    packed = jnp.concatenate(
        [
            w_bc.astype(F32),
            norm_gain.astype(F32).reshape(-1, bc_here),
            conv_bc,
            conv_bc_bias[None],
            jnp.full((1, bc_here), largest),
        ],
        axis=0,
    )
    packed = lax.all_gather(packed, "head")
    w_dt, w_bc, w_out = after((w_dt, w_bc, w_out), hidden)
    gain_end = full_width + part_width // bc_here
    w_bc_all = jnp.concatenate([packed[j, :full_width] for j in range(4)], axis=1).astype(BF)
    gain_all = packed[:, full_width:gain_end].reshape(4, part_width)
    gain_here = jnp.concatenate(
        [lax.dynamic_slice_in_dim(gain_all, index[k], 1, 0) for k in range(4)], axis=0
    )
    taps_bc_own = jnp.concatenate([conv_bc, conv_bc_bias[None], jnp.zeros((3, bc_here), F32)])
    taps_bc = jnp.concatenate([packed[j, gain_end : gain_end + 5] for j in range(4)], axis=1)
    out_scale = 16.0 / jnp.maximum(jnp.max(packed[:, gain_end + 5, 0]), 1e-30)
    taps_x = jnp.concatenate([conv_x, conv_x_bias[None]])
    taps = jnp.pad(jnp.concatenate([taps_x, taps_bc], axis=1), ((0, 3), (0, 0)))
    w_dt_wide = jnp.pad(w_dt, ((0, 0), (0, LANES - heads)))
    w_rest = jnp.concatenate([w_bc_all, w_dt_wide], axis=1)
    w_back = jnp.concatenate([w_z, w_x, w_dt_wide], axis=1).T
    w_bc_back = w_bc.T
    w_out_back = w_out.T
    w_out_parts = [
        lax.dynamic_slice_in_dim(w_out, index[k] * part_width, part_width, 1) for k in range(4)
    ]
    dt_params = jnp.pad(jnp.stack([dt_bias, a_log]), ((0, 6), (0, LANES - heads)))
    skip_wide = jnp.repeat(skip, HEAD_DIM)[None]
    gate_wide = gate_gain[None]
    owner = np.arange(inner) // HEAD_DIM
    spread = jnp.asarray(np.arange(LANES)[:, None] == owner[None, :], BF)
    collect = jnp.asarray(owner[:, None] == np.arange(LANES)[None, :], BF)
    order = np.arange(CHUNK)
    lower = jnp.asarray(order[:, None] >= order[None, :], BF)
    upper = jnp.asarray(order[:, None] <= order[None, :], BF)

    tokens = []
    near = [swap(hidden[0], 1), swap(hidden[0], 2)]
    pieces = exchange(after(out_grad, near).reshape((shards, each) + out_grad.shape[1:]), z)
    near, gain_here, w_rest, taps, w_out_back, w_back = after(
        (near, gain_here, w_rest, taps, w_out_back, w_back), hidden
    )
    near = after(near, gain_here, w_rest, taps, w_out_back, w_back)
    for s in range(each):
        own = hidden[s]
        if s:
            own = after(own, near)
            near = [swap(own, 1), swap(own, 2)]
        tokens.append([own] + near + [far_features(*near)])
    straight = jnp.arange(4, dtype=jnp.int32)

    x_specs = [rows_spec(part_width)] * 4
    x_flipped = [rows_spec(part_width, chunks)] * 4
    g_specs = [
        pl.BlockSpec((None, CHUNK, part_width), lambda c, k=k: (k, c, 0)) for k in range(4)
    ]
    gain_spec = whole_spec((4, part_width))
    rows_inner = rows_spec(inner)

    forward = call(
        forward_kernel,
        "forward_scan",
        chunks,
        [SCALARS] + x_specs + [
            whole_spec(w_z.shape), whole_spec(w_x.shape), whole_spec(w_rest.shape), gain_spec,
            whole_spec(taps.shape), whole_spec((8, LANES)),
            whole_spec((1, inner)), whole_spec(spread.shape), whole_spec(lower.shape),
        ],
        [
            (rows_inner, (length, inner), F32),
            (rows_spec(tail_width), (length, tail_width), F32),
            (rows_inner, (length, inner), F32),
            (pl.BlockSpec((None, inner, STATE), lambda c: (c, 0, 0)), (chunks, inner, STATE), F32),
        ],
        [pltpu.VMEM((CHUNK + 8, conv_width), F32), pltpu.VMEM((inner, STATE), F32)],
        10**9, 10**7,
    )
    ahead = [
        forward(index, *x, w_z, w_x, w_rest, gain_here, taps, dt_params, skip_wide, spread, lower)
        for x in tokens
    ]
    own_cot = in_order(after(pieces, ahead[0][0], tokens[-1][1]), z, 1)
    own_cot = [own_cot[s] for s in range(each)]
    cotangents = [lax.all_gather(own, "head") for own in own_cot]

    score = call(
        score_kernel,
        "gate_sums",
        chunks,
        [SCALARS] + g_specs + [
            whole_spec(w_out_back.shape), rows_inner, rows_inner, whole_spec((1, inner)),
        ],
        [(rows_inner, (length, inner), F32), (sums_spec(), (chunks, 8, CHUNK), F32)],
        [],
        10**9, 10**6,
    )
    flipped = rows_spec(inner, chunks)
    backward = call(
        functools.partial(backward_kernel, inner * lax.axis_size("head")),
        "backward_scan",
        chunks,
        [SCALARS] + [sums_spec(chunks)] * 4 + [
            flipped, flipped, flipped, rows_spec(tail_width, chunks),
            before_spec(tail_width, chunks),
            pl.BlockSpec((None, inner, STATE), lambda c: (chunks - 1 - c, 0, 0)),
            whole_spec((1, inner)), whole_spec(taps.shape), whole_spec((8, LANES)),
            whole_spec((1, inner)), whole_spec(spread.shape), whole_spec(collect.shape),
            whole_spec(lower.shape), whole_spec(upper.shape),
        ],
        [
            (flipped, (length, inner), BF),
            (flipped, (length, inner), BF),
            (flipped, (length, inner), BF),
            (rows_spec(LANES, chunks), (length, LANES), BF),
            (rows_spec(2 * STATE, chunks), (length, 2 * STATE), F32),
            (whole_spec((8, inner)), (8, inner), F32),
            (whole_spec((8, LANES)), (8, LANES), F32),
        ],
        [
            pltpu.VMEM((CHUNK + 8, conv_width), F32),
            pltpu.VMEM((CHUNK + 8, inner), F32),
            pltpu.VMEM((inner, STATE), F32),
        ],
        2 * 10**9, 10**7,
    )
    sum_shapes = [(full_width, 2 * inner), (full_width, LANES), (inner, full_width)]

    def weigh(*args):
        return call(
            weight_kernel,
            "weight_sums",
            chunks,
            [SCALARS] + x_specs + g_specs + [
                gain_spec, whole_spec(w_back.shape), rows_inner, rows_inner, rows_inner,
                rows_spec(LANES),
            ] + [whole_spec(shape) for shape in sum_shapes[: len(args) - 15]],
            [(rows_spec(full_width), (length, full_width), F32)]
            + [(whole_spec(shape), shape, F32) for shape in sum_shapes],
            [],
            2 * 10**9, 10**7,
        )(*args)

    mix = call(
        mixed_kernel,
        "input_sums",
        chunks,
        [SCALARS] + x_flipped + [gain_spec, whole_spec(w_bc_back.shape)]
        + [rows_spec(bc_here, chunks)] * 2
        + [before_spec(bc_here, chunks), whole_spec((8, bc_here)), rows_spec(full_width, chunks)],
        [
            (part_spec(8, part_width, chunks), (chunks, CHUNK + 8, part_width), F32),
            (part_spec(16, part_width, chunks), (chunks, CHUNK + 16, part_width), BF),
            (part_spec(16, part_width, chunks), (chunks, CHUNK + 16, part_width), BF),
            (part_spec(16, part_width, chunks), (chunks, CHUNK + 16, part_width), BF),
            (whole_spec((full_width, bc_here)), (full_width, bc_here), F32),
            (whole_spec((8, bc_here)), (8, bc_here), F32),
        ],
        [pltpu.VMEM((CHUNK + 8, bc_here), F32), pltpu.VMEM((CHUNK + 8, bc_here), F32)],
        10**9, 10**7,
    )
    finish = call(
        final_kernel,
        "input_gradient",
        chunks,
        x_specs + [gain_spec, part_spec(8, part_width)] + [part_spec(16, part_width)] * 3
        + [rows_spec(part_width)],
        [
            (rows_spec(part_width), (length, part_width), F32),
            (whole_spec((8, part_width)), (8, part_width), F32),
        ],
        [],
        10**8, 10**6,
    )

    def scores_of(s, cotangent):
        gate, _, ssd, _ = ahead[s]
        d_scaled, sums = score(straight, *[cotangent] * 4, w_out_back, ssd, gate, gate_wide)
        return d_scaled, [sums] + [swap(sums, k) for k in range(1, 4)]

    behind, d_bc_all, blocks, outward = [], [], [], []
    for s in range(each):
        gate, conv, ssd, states = ahead[s]
        cotangent = after(cotangents[s], behind[-1][0]) if behind else cotangents[s]
        d_scaled, sums = scores_of(s, cotangent)
        if behind:
            sums = after(sums, outward[-1])
        behind.append(
            backward(
                index, *sums, ssd, gate, d_scaled, conv, conv, states, gate_wide, taps, dt_params,
                skip_wide, spread, collect, lower, upper,
            )
        )
        d_bc = behind[s][4]
        power = exponent_of(jnp.max(jnp.abs(d_bc)))
        parts = [
            lax.dynamic_slice_in_dim(d_bc, index[k] * bc_here, bc_here, 1) for k in range(4)
        ]
        sent = [
            swap(to_half(jnp.concatenate([p[: length // 2], p[length // 2 :]], axis=1), power), k)
            for k, p in enumerate(parts)
            if k
        ]
        total = sum(from_half(part)[0] for part in sent)
        total = jnp.concatenate([total[:, :bc_here], total[:, bc_here:]], axis=0)
        d_bc_all.append(parts[0] + total)

        scaled = behind[s][0]
        out_parts = [jnp.dot(scaled, part, preferred_element_type=F32) for part in w_out_parts]
        outward.append([(out_parts[k] * out_scale).astype(jnp.float16) for k in range(1, 4)])
        received = [swap(part, k + 1) for k, part in enumerate(after(outward[s], sent))]
        block = tokens[s][0].astype(F32) + out_parts[0]
        blocks.append((block + sum(part.astype(F32) for part in received) / out_scale).astype(BF))

    g_sums, mixed = [], []
    sent_blocks = [to_tokens(block, z) for block in blocks]
    for s in range(each):
        scaled, d_gate, d_x, d_dt, _, _, _ = behind[s]
        if s == 0:
            d_dt = after(d_dt, outward, blocks[:-1])
        else:
            d_dt = after(d_dt, mixed[-1][0])
        d_normed, *g_sums = weigh(
            index, *tokens[s], *[cotangents[s]] * 4, gain_here, w_back, scaled, d_gate, d_x, d_dt,
            *g_sums,
        )
        if s + 1 == each:
            d_normed = after(d_normed, sent_blocks[:-1], blocks[-1])
        conv_own = lax.dynamic_slice_in_dim(ahead[s][1], inner + me * bc_here, bc_here, 1)
        own, send1, send2, send3, g_bc, taps_sums = mix(
            index, *tokens[s], gain_here, w_bc_back, d_bc_all[s], conv_own, conv_own, taps_bc_own,
            d_normed,
        )
        mixed.append((own, (swap(send1, 1), swap(send2, 2), swap(send3, 3)), g_bc, taps_sums))
    g_wide, g_dt, g_w_out = g_sums
    g_wide, g_w_out = lax.psum((g_wide, g_w_out), ("seq", "dp"))
    wide = sum(part[5] for part in behind)
    dt_sums = sum(part[6] for part in behind)

    grads, gain_sums = [], []
    for s in range(each):
        own, sends, _, _ = mixed[s]
        own = after(own, mixed[-1][0])
        grad, gain_sum = finish(*tokens[s], gain_here, own, *sends, own_cot[s])
        gain_sums.append(gain_sum[0:1])
        grads.append(to_tokens(grad, z, jnp.max(gain_sum[1])))
    g_bc = sum(part[2] for part in mixed)
    taps_sums = sum(part[3] for part in mixed)
    gain_sums = sum(gain_sums)
    late = [
        part.reshape(-1, LANES)
        for part in (g_bc, g_dt[:, :heads], wide, dt_sums, taps_sums, gain_sums)
    ]
    ends = np.cumsum([0] + [part.shape[0] for part in late])
    late = butterfly_sum(jnp.concatenate(late, axis=0))
    late = [late[ends[i] : ends[i + 1]] for i in range(len(ends) - 1)]
    g_bc, g_dt, wide, dt_sums, taps_sums, gain_sums = late
    g_bc = g_bc.reshape(full_width, bc_here)
    g_dt = g_dt.reshape(full_width, heads)
    wide = wide.reshape(8, inner)
    taps_sums = taps_sums.reshape(8, bc_here)
    gain_sums = gain_sums.reshape(1, part_width)
    return (
        joined_tokens(sent_blocks),
        joined_tokens(grads),
        gain_sums[0],
        g_wide[:, :inner],
        g_wide[:, inner:],
        g_bc,
        g_dt,
        wide[0:4],
        wide[4],
        taps_sums[0:4],
        taps_sums[4],
        dt_sums[1, :heads],
        dt_sums[0, :heads],
        wide[6].reshape(heads, HEAD_DIM).sum(axis=1),
        wide[5],
        g_w_out,
    )


def fits(mesh, seqs, length):
    shards = mesh.shape["seq"]
    local_seqs = seqs // mesh.shape["dp"]
    doubling = all(mesh.shape[axis] & (mesh.shape[axis] - 1) == 0 for axis in ("seq", "dp"))
    return doubling and mesh.shape["head"] == 4 and local_seqs % shards == 0 and length % CHUNK == 0


def solution(mesh):
    in_specs = (
        P("dp", "seq", "head"),
        P("head"),
        P(None, "head"),
        P(None, "head"),
        P(None, "head"),
        P(None, "head"),
        P(None, "head"),
        P("head"),
        P(None, "head"),
        P("head"),
        P("head"),
        P("head"),
        P("head"),
        P("head"),
        P("head", None),
        P("dp", "seq", "head"),
    )
    out_specs = (
        P("dp", "seq", "head"),
        P("dp", "seq", "head"),
        P("head"),
        P(None, "head"),
        P(None, "head"),
        P(None, "head"),
        P(None, "head"),
        P(None, "head"),
        P("head"),
        P(None, "head"),
        P("head"),
        P("head"),
        P("head"),
        P("head"),
        P("head"),
        P("head", None),
    )

    def run(*args):
        seqs, length, _ = args[0].shape
        body = on_device if fits(mesh, seqs, length) else on_device_general
        return jax.shard_map(
            body, mesh=mesh, in_specs=in_specs, out_specs=out_specs, check_vma=False
        )(*args)

    return run
```

```python
import functools
import jax
import jax.numpy as jnp
import numpy as np
from jax import lax
from jax.experimental import pallas as pl
from jax.experimental.pallas import tpu as pltpu
from jax.sharding import PartitionSpec as P

HEAD_DIM = 64
STATE = 128


epsilon = 1e-05
highest = lax.Precision.HIGHEST


def from_behind(value, axis, steps):
    count = lax.axis_size(axis)
    leading, last = (max(0, -steps), min(count, count - steps))
    return lax.ppermute(value, axis, [(source, source + steps) for source in range(leading, last)])


def prefix(value, axis, join, neutral, backward):
    count, mine = (lax.axis_size(axis), lax.axis_index(axis))
    pieces = jax.tree.map(lambda part: lax.all_gather(part, axis), value)
    if backward:
        pieces = jax.tree.map(lambda part: part[::-1], pieces)
        mine = count - 1 - mine
    total = jax.tree.map(
        lambda part, zero: jnp.full_like(part, 0) + jnp.asarray(zero, part.dtype), value, neutral
    )

    def turn(position, total):
        longer = join(total, jax.tree.map(lambda part: part[position], pieces))
        return jax.tree.map(lambda new, old: jnp.where(position < mine, new, old), longer, total)

    return lax.fori_loop(0, count - 1, turn, total)


def silu_grad(pre_value):
    gate_sig = jax.nn.sigmoid(pre_value)
    return gate_sig * (1.0 + pre_value * (1.0 - gate_sig))


def chain_step(earlier, later):
    return (earlier[0] + later[0], earlier[1] * jnp.exp(later[0])[:, :, None, None] + later[1])


def on_device_general(
    hidden_in,
    norm_gain,
    w_z,
    w_x,
    w_bc,
    w_dt,
    conv_x,
    conv_x_bias,
    conv_bc,
    conv_bc_bias,
    dt_bias,
    a_log,
    skip,
    gate_gain,
    w_out,
    out_grad,
):
    seq_count, local_len, part_width = hidden_in.shape
    heads_here = dt_bias.shape[0]
    inner_here = w_x.shape[1]
    bc_here = w_bc.shape[1]
    kernel_span = conv_x.shape[0]
    edge_len = kernel_span - 1
    row_count = seq_count * local_len
    whole_x, whole_cot, whole_gain = (
        lax.all_gather(hidden_in, "head", axis=2, tiled=True),
        lax.all_gather(out_grad, "head", axis=2, tiled=True),
        lax.all_gather(norm_gain, "head", axis=0, tiled=True),
    )
    full_width = whole_x.shape[2]
    x_full = whole_x.astype(jnp.float32)
    inv_rms = lax.rsqrt(jnp.mean(x_full * x_full, axis=-1, keepdims=True) + epsilon)
    normed = (
        (x_full * inv_rms * whole_gain.astype(jnp.float32))
        .astype(jnp.bfloat16)
        .reshape(row_count, full_width)
    )
    w_cat = jnp.concatenate([w_z, w_x, w_bc, w_dt], axis=1)
    projected = jnp.dot(normed, w_cat, preferred_element_type=jnp.float32).reshape(
        seq_count, local_len, -1
    )
    conv_end = 2 * inner_here + bc_here
    gate_pre = projected[:, :, :inner_here]
    conv_in = projected[:, :, inner_here:conv_end]
    dt_raw = projected[:, :, conv_end:]
    edge_in = from_behind(conv_in[:, local_len - edge_len :, :], "seq", 1)
    extended = jnp.concatenate([edge_in, conv_in], axis=1)
    kernel = jnp.concatenate([conv_x, conv_bc], axis=1)
    kernel_bias = jnp.concatenate([conv_x_bias, conv_bc_bias], axis=0)
    pre_act = jnp.broadcast_to(kernel_bias, conv_in.shape)
    for tap_index in range(kernel_span):
        pre_act = pre_act + kernel[tap_index] * extended[:, tap_index : tap_index + local_len]
    activated = jax.nn.silu(pre_act)
    x_conv = activated[:, :, :inner_here].astype(jnp.bfloat16)
    bc_all = lax.all_gather(
        activated[:, :, inner_here:].astype(jnp.bfloat16), "head", axis=2, tiled=True
    )
    b_rows = bc_all[:, :, :STATE].astype(jnp.float32)
    c_rows = bc_all[:, :, STATE:].astype(jnp.float32)
    values = x_conv.astype(jnp.float32).reshape(seq_count, local_len, heads_here, HEAD_DIM)
    step_size = jax.nn.softplus(dt_raw + dt_bias)
    decay_rate = -jnp.exp(a_log)
    step_log = step_size * decay_rate
    cumulative = jnp.cumsum(step_log, axis=1)
    total_log = cumulative[:, -1, :]
    cum_heads = cumulative.transpose(0, 2, 1)
    step_heads = step_size.transpose(0, 2, 1)
    causal = jnp.arange(local_len)[:, None] >= jnp.arange(local_len)[None, :]
    gap_log = cum_heads[:, :, :, None] - cum_heads[:, :, None, :]
    decay_mat = jnp.where(causal, jnp.exp(jnp.where(causal, gap_log, 0.0)), 0.0)
    scores = jnp.einsum("btn,bsn->bts", c_rows, b_rows, precision=highest)
    decayed = scores[:, None, :, :] * decay_mat
    weights = decayed * step_heads[:, :, None, :]
    local_out = jnp.einsum("bhts,bshp->bthp", weights, values, precision=highest)
    carry_scale = jnp.exp(total_log[:, None, :] - cumulative)
    carry_weight = carry_scale * step_size
    weighted_values = values * carry_weight[..., None]
    local_state = jnp.einsum("bshp,bsn->bhpn", weighted_values, b_rows, precision=highest)
    empty = (jnp.zeros_like(total_log), jnp.zeros_like(local_state))
    _, state_in = prefix((total_log, local_state), "seq", chain_step, empty, False)
    cum_exp = jnp.exp(cumulative)
    cross_out = cum_exp[..., None] * jnp.einsum(
        "btn,bhpn->bthp", c_rows, state_in, precision=highest
    )
    ssd_out = (local_out + cross_out + skip[:, None] * values).reshape(
        seq_count, local_len, inner_here
    )
    gate_act = jax.nn.silu(gate_pre)
    gated_out = ssd_out * gate_act
    inner_width = inner_here * lax.axis_size("head")
    square_sum = lax.psum(jnp.sum(gated_out * gated_out, axis=-1), "head")
    gate_rms = lax.rsqrt(square_sum / inner_width + epsilon)[..., None]
    scaled = (gated_out * gate_rms * gate_gain).astype(jnp.bfloat16).reshape(row_count, inner_here)
    out_own = lax.psum_scatter(
        lax.dot_general(
            w_out, scaled, (((0,), (1,)), ((), ())), preferred_element_type=jnp.float32
        ),
        "head",
        scatter_dimension=0,
        tiled=True,
    )
    x_own = hidden_in.astype(jnp.float32)
    block_out = (x_own + out_own.T.reshape(seq_count, local_len, part_width)).astype(jnp.bfloat16)
    cot_rows = whole_cot.reshape(row_count, full_width)
    g_w_out = lax.dot_general(
        scaled, cot_rows, (((0,), (0,)), ((), ())), preferred_element_type=jnp.float32
    )
    d_scaled = lax.dot_general(
        cot_rows, w_out, (((1,), (1,)), ((), ())), preferred_element_type=jnp.float32
    )
    d_scaled = d_scaled.reshape(seq_count, local_len, inner_here)
    g_gate_gain = jnp.sum(d_scaled * gated_out * gate_rms, axis=(0, 1))
    gain_term = d_scaled * gate_gain
    inner_dot = lax.psum(jnp.sum(gain_term * gated_out, axis=-1), "head")
    d_gated = gate_rms * gain_term - gated_out * gate_rms**3 * (inner_dot / inner_width)[..., None]
    d_gate = d_gated * ssd_out * silu_grad(gate_pre)
    d_out = (d_gated * gate_act).reshape(seq_count, local_len, heads_here, HEAD_DIM)
    g_skip = jnp.sum(d_out * values, axis=(0, 1, 3))
    gram = jnp.einsum("bthp,bshp->bhts", d_out, values, precision=highest)
    d_values = (
        jnp.einsum("bhts,bthp->bshp", weights, d_out, precision=highest) + skip[:, None] * d_out
    )
    masked = gram * decayed
    d_scores = jnp.sum(gram * decay_mat * step_heads[:, :, None, :], axis=1)
    d_step_intra = jnp.sum(masked, axis=2).transpose(0, 2, 1)
    d_gap = masked * step_heads[:, :, None, :]
    d_cum_intra = (jnp.sum(d_gap, axis=3) - jnp.sum(d_gap, axis=2)).transpose(0, 2, 1)
    d_c = jnp.einsum("bts,bsn->btn", d_scores, b_rows, precision=highest)
    d_b = jnp.einsum("bts,btn->bsn", d_scores, c_rows, precision=highest)
    d_out_exp = d_out * cum_exp[..., None]
    d_c = d_c + jnp.einsum("bthp,bhpn->btn", d_out_exp, state_in, precision=highest)
    d_state_in = jnp.einsum("bthp,btn->bhpn", d_out_exp, c_rows, precision=highest)
    d_cum_cross = jnp.sum(d_out * cross_out, axis=3)
    _, d_local_state = prefix((total_log, d_state_in), "seq", chain_step, empty, True)
    state_back = jnp.einsum("bhpn,bsn->bshp", d_local_state, b_rows, precision=highest)
    d_values = d_values + carry_weight[..., None] * state_back
    d_b = d_b + jnp.einsum("bshp,bhpn->bsn", weighted_values, d_local_state, precision=highest)
    d_carry = jnp.sum(values * state_back, axis=3)
    carry_prod = d_carry * carry_weight
    d_total = jnp.exp(total_log) * jnp.sum(state_in * d_local_state, axis=(2, 3)) + jnp.sum(
        carry_prod, axis=1
    )
    d_cum = d_cum_intra + d_cum_cross - carry_prod
    d_cum = d_cum.at[:, -1, :].add(d_total)
    d_step_log = jnp.cumsum(d_cum[:, ::-1, :], axis=1)[:, ::-1, :]
    d_step = d_step_intra + d_carry * carry_scale + d_step_log * decay_rate
    g_a_log = jnp.sum(d_step_log * step_log, axis=(0, 1))
    d_dt_pre = d_step * jax.nn.sigmoid(dt_raw + dt_bias)
    g_dt_bias = jnp.sum(d_dt_pre, axis=(0, 1))
    d_bc_own = lax.psum_scatter(
        jnp.concatenate([d_b, d_c], axis=2), "head", scatter_dimension=2, tiled=True
    )
    d_act = jnp.concatenate([d_values.reshape(seq_count, local_len, inner_here), d_bc_own], axis=2)
    d_pre = d_act * silu_grad(pre_act)
    g_kernel = jnp.stack(
        [
            jnp.sum(d_pre * extended[:, tap_index : tap_index + local_len], axis=(0, 1))
            for tap_index in range(kernel_span)
        ]
    )
    g_kernel_bias = jnp.sum(d_pre, axis=(0, 1))
    d_padded = jnp.pad(d_pre, ((0, 0), (edge_len, edge_len), (0, 0)))
    d_ext = jnp.zeros_like(extended)
    for tap_index in range(kernel_span):
        offset = edge_len - tap_index
        d_ext = d_ext + kernel[tap_index] * d_padded[:, offset : offset + local_len + edge_len]
    back_edge = from_behind(d_ext[:, :edge_len, :], "seq", -1)
    d_conv_in = d_ext[:, edge_len:, :].at[:, local_len - edge_len :, :].add(back_edge)
    d_proj = (
        jnp.concatenate([d_gate, d_conv_in, d_dt_pre], axis=2)
        .astype(jnp.bfloat16)
        .reshape(row_count, -1)
    )
    g_w_cat = lax.dot_general(
        normed, d_proj, (((0,), (0,)), ((), ())), preferred_element_type=jnp.float32
    )
    x_hat_own = x_own * inv_rms
    gain_own = norm_gain.astype(jnp.float32)
    d_own = lax.psum_scatter(
        lax.dot_general(
            w_cat, d_proj, (((1,), (1,)), ((), ())), preferred_element_type=jnp.float32
        ),
        "head",
        scatter_dimension=0,
        tiled=True,
    ).T.reshape(seq_count, local_len, part_width)
    d_hat_own = d_own * gain_own
    row_mean = lax.psum(jnp.sum(d_hat_own * x_hat_own, axis=-1), "head")[..., None] / full_width
    grad_in = out_grad.astype(jnp.float32) + inv_rms * (d_hat_own - x_hat_own * row_mean)
    g_norm_gain = jnp.sum(d_own * x_hat_own, axis=(0, 1))
    (
        g_norm_gain,
        g_w_cat,
        g_kernel,
        g_kernel_bias,
        g_dt_bias,
        g_a_log,
        g_skip,
        g_gate_gain,
        g_w_out,
    ) = lax.psum(
        (
            g_norm_gain,
            g_w_cat,
            g_kernel,
            g_kernel_bias,
            g_dt_bias,
            g_a_log,
            g_skip,
            g_gate_gain,
            g_w_out,
        ),
        ("seq", "dp"),
    )
    g_w_z = g_w_cat[:, :inner_here]
    g_w_x = g_w_cat[:, inner_here : 2 * inner_here]
    g_w_bc = g_w_cat[:, 2 * inner_here : conv_end]
    g_w_dt = g_w_cat[:, conv_end:]
    return (
        block_out,
        grad_in,
        g_norm_gain,
        g_w_z,
        g_w_x,
        g_w_bc,
        g_w_dt,
        g_kernel[:, :inner_here],
        g_kernel_bias[:inner_here],
        g_kernel[:, inner_here:],
        g_kernel_bias[inner_here:],
        g_dt_bias,
        g_a_log,
        g_skip,
        g_gate_gain,
        g_w_out,
    )


BF = jnp.bfloat16
F32 = jnp.float32
CHUNK = 256
LANES = 128
VMEM_LIMIT = 56 * 1024 * 1024


def dot_nn(a, b):
    return lax.dot_general(a, b, (((1,), (0,)), ((), ())), preferred_element_type=F32)


def dot_nt(a, b):
    return lax.dot_general(a, b, (((1,), (1,)), ((), ())), preferred_element_type=F32)


def dot_tn(a, b):
    return lax.dot_general(a, b, (((0,), (0,)), ((), ())), preferred_element_type=F32)


def split2(value):
    high = value.astype(BF)
    return high, (value - high.astype(F32)).astype(BF)


def split3(value):
    high = value.astype(BF)
    rest = value - high.astype(F32)
    middle = rest.astype(BF)
    return high, middle, (rest - middle.astype(F32)).astype(BF)


def sigmoid(value):
    return 1.0 / (1.0 + jnp.exp(-value))


def silu_slope(value, sig):
    return sig * (1.0 + value * (1.0 - sig))


def step_values(dt_block, dt_params):
    shifted = dt_block + dt_params[0:1]
    step = jnp.maximum(shifted, 0.0) + jnp.log1p(jnp.exp(-jnp.abs(shifted)))
    rate = -jnp.exp(dt_params[1:2])
    return shifted, step, rate, step * rate


def inverse_rms(blocks):
    total = sum(jnp.sum(block * block, axis=1, keepdims=True) for block in blocks)
    return lax.rsqrt(total / (len(blocks) * blocks[0].shape[1]) + epsilon)


def normed_blocks(x_refs, gain_ref):
    blocks = [ref[...].astype(F32) for ref in x_refs]
    inverse = inverse_rms(blocks)
    hats = [block * inverse for block in blocks]
    return inverse, hats, [(hat * gain_ref[k : k + 1]).astype(BF) for k, hat in enumerate(hats)]


def block_of(index_ref, k, size):
    return pl.ds(pl.multiple_of(index_ref[k] * size, size), size)


def column_of_sums(rows, lanes_here):
    tile = jnp.zeros((CHUNK, LANES), F32)
    lane = lax.broadcasted_iota(jnp.int32, (CHUNK, LANES), 1)
    for position, value in enumerate(rows):
        tile = jnp.where(lane == position, value, tile)
    return jnp.transpose(tile)[0:lanes_here]


def forward_kernel(
    index_ref, x0, x1, x2, x3, w_z_ref, w_x_ref, w_rest_ref, gain_ref, taps_ref, dt_ref, skip_ref,
    spread_ref, lower_ref, gate_out, conv_out, ssd_out, state_out, extended, state,
):
    inner = skip_ref.shape[1]
    heads = inner // HEAD_DIM
    conv_width = inner + 2 * STATE

    @pl.when(pl.program_id(0) == 0)
    def _():
        extended[0:8, :] = jnp.zeros((8, conv_width), F32)
        state[...] = jnp.zeros(state.shape, F32)

    x_refs = (x0, x1, x2, x3)
    _, _, normed = normed_blocks(x_refs, gain_ref)
    parts = [block_of(index_ref, k, part.shape[1]) for k, part in enumerate(normed)]
    gate_out[...] = sum(dot_nn(part, w_z_ref[rows, :]) for part, rows in zip(normed, parts))
    projected = jnp.concatenate(
        [
            sum(dot_nn(part, ref[rows, :]) for part, rows in zip(normed, parts))
            for ref in (w_x_ref, w_rest_ref)
        ],
        axis=1,
    )
    conv_out[...] = projected
    conv_in = projected[:, :conv_width]
    extended[8 : 8 + CHUNK, :] = conv_in
    pre_act = taps_ref[4:5, :] + taps_ref[3:4, :] * conv_in
    for k in range(3):
        pre_act = pre_act + taps_ref[k : k + 1, :] * extended[5 + k : 5 + k + CHUNK, :]
    extended[0:8, :] = conv_in[CHUNK - 8 :, :]
    act = (pre_act * sigmoid(pre_act)).astype(BF)
    values = act[:, :inner]
    b_rows = act[:, inner : inner + STATE]
    c_rows = act[:, inner + STATE :]

    _, step, _, step_log = step_values(projected[:, conv_width:], dt_ref)
    cumulative = sum(dot_nn(lower_ref[...], part) for part in split3(step_log))
    cum_t = jnp.transpose(cumulative)
    step_t = jnp.transpose(step)
    total = cumulative[CHUNK - 1 : CHUNK, :]
    spread = spread_ref[...]
    widened = jnp.concatenate([jnp.exp(cumulative), jnp.exp(total - cumulative) * step], axis=0)
    high, low = split2(widened)
    widened = dot_nn(high, spread) + dot_nn(low, spread)
    cum_exp, carry_weight = widened[:CHUNK], widened[CHUNK:]

    state_now = state[...]
    state_out[...] = state_now
    s_high, s_low = split2(state_now)
    cross = dot_nt(c_rows, s_high) + dot_nt(c_rows, s_low)
    values_f = values.astype(F32)
    carried = cum_exp * cross + skip_ref[...] * values_f

    scores = dot_nt(c_rows, b_rows)
    row = lax.broadcasted_iota(jnp.int32, (CHUNK, CHUNK), 0)
    column = lax.broadcasted_iota(jnp.int32, (CHUNK, CHUNK), 1)
    causal = row >= column
    lane = lax.broadcasted_iota(jnp.int32, (CHUNK, LANES), 1)
    for pair in range(heads // 2):
        lanes = slice(pair * LANES, (pair + 1) * LANES)
        total_out = carried[:, lanes]
        for side in range(2):
            h = 2 * pair + side
            mine = (lane >= HEAD_DIM) if side else (lane < HEAD_DIM)
            own_values = jnp.where(mine, values[:, lanes], jnp.zeros((), BF))
            gap = cumulative[:, h : h + 1] - cum_t[h : h + 1, :]
            decay = jnp.exp(jnp.where(causal, gap, -1e30))
            high, low = split2(scores * decay * step_t[h : h + 1, :])
            total_out = total_out + dot_nn(high, own_values) + dot_nn(low, own_values)
        ssd_out[:, lanes] = total_out

    high, low = split2(values_f * carry_weight)
    grown = dot_tn(high, b_rows) + dot_tn(low, b_rows)
    total_t = jnp.exp(cum_t[:, CHUNK - 1 : CHUNK])
    for h in range(heads):
        part = slice(h * HEAD_DIM, (h + 1) * HEAD_DIM)
        state[part, :] = total_t[h : h + 1, :] * state_now[part] + grown[part]


def score_kernel(index_ref, g0, g1, g2, g3, w_ref, ssd_ref, gate_ref, gain_ref, d_out, sums_out):
    d_scaled = sum(
        dot_nn(ref[...], w_ref[block_of(index_ref, k, ref.shape[1]), :])
        for k, ref in enumerate((g0, g1, g2, g3))
    )
    d_out[...] = d_scaled
    gate = gate_ref[...]
    gated = ssd_ref[...] * (gate * sigmoid(gate))
    squares = jnp.sum(gated * gated, axis=1, keepdims=True)
    inner_dot = jnp.sum(d_scaled * gain_ref[...] * gated, axis=1, keepdims=True)
    sums_out[0] = column_of_sums((squares, inner_dot), 8)


def backward_kernel(
    inner_width, index_ref, q0, q1, q2, q3, ssd_ref, gate_ref, d_scaled_ref, conv_ref, before_ref,
    state_ref, gain_ref, taps_ref, dt_ref, skip_ref, spread_ref, gather_ref, lower_ref, upper_ref,
    scaled_out, d_gate_out, d_x_out, d_dt_out, d_bc_out, wide_out, dt_out,
    extended, d_pre, state_grad,
):
    inner = skip_ref.shape[1]
    heads = inner // HEAD_DIM
    conv_width = inner + 2 * STATE
    step_at = pl.program_id(0)
    chunk_at = pl.num_programs(0) - 1 - step_at

    @pl.when(step_at == 0)
    def _():
        d_pre[CHUNK : CHUNK + 8, :] = jnp.zeros((8, inner), F32)
        state_grad[...] = jnp.zeros(state_grad.shape, F32)
        wide_out[...] = jnp.zeros(wide_out.shape, F32)
        dt_out[...] = jnp.zeros(dt_out.shape, F32)

    sums = q0[0] + q1[0] + q2[0] + q3[0]
    sums = jnp.transpose(jnp.concatenate([sums, jnp.zeros((LANES - 8, CHUNK), F32)], axis=0))
    rms = lax.rsqrt(sums[:, 0:1] / inner_width + epsilon)
    mean_dot = sums[:, 1:2] / inner_width
    gate = gate_ref[...]
    gate_sig = sigmoid(gate)
    gate_act = gate * gate_sig
    ssd = ssd_ref[...]
    gated = ssd * gate_act
    gated_rms = gated * rms
    gain = gain_ref[...]
    d_scaled = d_scaled_ref[...]
    scaled_out[...] = (gated_rms * gain).astype(BF)
    wide_out[5:6, :] += jnp.sum(d_scaled * gated_rms, axis=0, keepdims=True)
    d_gated = rms * (d_scaled * gain) - gated * (rms * rms * rms * mean_dot)
    d_gate_out[...] = (d_gated * ssd * silu_slope(gate, gate_sig)).astype(BF)
    d_ssd = d_gated * gate_act

    conv_in = conv_ref[:, :conv_width]
    extended[0:8, :] = jnp.where(chunk_at > 0, before_ref[:, :conv_width], 0.0)
    extended[8 : 8 + CHUNK, :] = conv_in
    pre_act = taps_ref[4:5, :] + taps_ref[3:4, :] * conv_in
    for k in range(3):
        pre_act = pre_act + taps_ref[k : k + 1, :] * extended[5 + k : 5 + k + CHUNK, :]
    sig = sigmoid(pre_act)
    act = (pre_act * sig).astype(BF)
    slope_x = silu_slope(pre_act[:, :inner], sig[:, :inner])
    values = act[:, :inner]
    values_f = values.astype(F32)
    b_rows = act[:, inner : inner + STATE]
    c_rows = act[:, inner + STATE :]
    wide_out[6:7, :] += jnp.sum(d_ssd * values_f, axis=0, keepdims=True)

    shifted, step, rate, step_log = step_values(conv_ref[:, conv_width:], dt_ref)
    cumulative = sum(dot_nn(lower_ref[...], part) for part in split3(step_log))
    cum_t = jnp.transpose(cumulative)
    total = cumulative[CHUNK - 1 : CHUNK, :]
    carry_scale = jnp.exp(total - cumulative)
    carry = carry_scale * step
    spread = spread_ref[...]
    high, low = split2(jnp.concatenate([jnp.exp(cumulative), carry], axis=0))
    widened = dot_nn(high, spread) + dot_nn(low, spread)
    cum_exp, carry_weight = widened[:CHUNK], widened[CHUNK:]

    scores = dot_nt(b_rows, c_rows)
    row = lax.broadcasted_iota(jnp.int32, (CHUNK, CHUNK), 0)
    column = lax.broadcasted_iota(jnp.int32, (CHUNK, CHUNK), 1)
    causal = row <= column
    lane = lax.broadcasted_iota(jnp.int32, (CHUNK, LANES), 1)

    s_high, s_low = split2(state_ref[...])
    r_now = state_grad[...]
    r_high, r_low = split2(r_now)
    cross = cum_exp * (dot_nt(c_rows, s_high) + dot_nt(c_rows, s_low))
    back = dot_nt(b_rows, r_high) + dot_nt(b_rows, r_low)
    d_values = carry_weight * back + skip_ref[...] * d_ssd

    d_scores = jnp.zeros((CHUNK, CHUNK), F32)
    step_intra = jnp.zeros((CHUNK, LANES), F32)
    row_sums = []
    d_parts = []
    for pair in range(heads // 2):
        lanes = slice(pair * LANES, (pair + 1) * LANES)
        g_high, g_low = split2(d_ssd[:, lanes])
        part = d_values[:, lanes]
        for side in range(2):
            h = 2 * pair + side
            mine = (lane >= HEAD_DIM) if side else (lane < HEAD_DIM)
            zero = jnp.zeros((), BF)
            own_values = jnp.where(mine, values[:, lanes], zero)
            own_high = jnp.where(mine, g_high, zero)
            own_low = jnp.where(mine, g_low, zero)
            gram = dot_nt(own_values, g_high) + dot_nt(own_values, g_low)
            gap = cum_t[h : h + 1, :] - cumulative[:, h : h + 1]
            decay = jnp.exp(jnp.where(causal, gap, -1e30))
            step_column = step[:, h : h + 1]
            pulled = gram * decay
            masked = pulled * scores
            d_scores = d_scores + pulled * step_column
            step_intra = jnp.where(
                lane == h, jnp.sum(masked, axis=1, keepdims=True), step_intra
            )
            row_sums.append(jnp.sum(masked * step_column, axis=0, keepdims=True))
            w_high, w_low = split2(scores * decay * step_column)
            part = part + dot_nn(w_high, own_high)
            part = part + dot_nn(w_low, own_high)
            part = part + dot_nn(w_high, own_low)
        d_parts.append(part)
    d_values = jnp.concatenate(d_parts, axis=1)

    high, low = split2(d_scores)
    d_b = dot_nn(high, c_rows) + dot_nn(low, c_rows)
    d_c = dot_tn(high, b_rows) + dot_tn(low, b_rows)
    d_ssd_exp = d_ssd * cum_exp
    e_high, e_low = split2(d_ssd_exp)
    d_c = d_c + dot_nn(e_high, s_high) + dot_nn(e_low, s_high) + dot_nn(e_high, s_low)
    weighted = values_f * carry_weight
    v_high, v_low = split2(weighted)
    d_b = d_b + dot_nn(v_high, r_high) + dot_nn(v_low, r_high) + dot_nn(v_high, r_low)
    d_bc_out[...] = jnp.concatenate([d_b, d_c], axis=1)

    gather = gather_ref[...]
    d_cum_cross = sum(dot_nn(p, gather) for p in split3(d_ssd * cross))
    d_carry = sum(dot_nn(p, gather) for p in split3(values_f * back))
    carry_prod = d_carry * carry
    kept = state_ref[...] * r_now
    kept = sum(dot_tn(gather, p) for p in split3(kept))
    kept = jnp.sum(kept, axis=1, keepdims=True)
    kept = jnp.transpose(jnp.broadcast_to(kept, (LANES, LANES)))[0:1]
    d_total = jnp.exp(total) * kept + jnp.sum(carry_prod, axis=0, keepdims=True)
    rows_t = jnp.concatenate(row_sums + [jnp.zeros((LANES - heads, CHUNK), F32)], axis=0)
    d_cum = jnp.transpose(rows_t) - step * step_intra + d_cum_cross - carry_prod
    last = lax.broadcasted_iota(jnp.int32, (CHUNK, LANES), 0) == CHUNK - 1
    d_cum = d_cum + jnp.where(last, d_total, 0.0)
    d_step_log = sum(dot_nn(upper_ref[...], p) for p in split3(d_cum))
    d_step = step_intra + d_carry * carry_scale + d_step_log * rate
    dt_out[0:1, :] += jnp.sum(d_step_log * step_log, axis=0, keepdims=True)
    d_dt = d_step * sigmoid(shifted)
    dt_out[1:2, :] += jnp.sum(d_dt, axis=0, keepdims=True)
    d_dt_out[...] = d_dt.astype(BF)

    grown = dot_tn(e_high, c_rows) + dot_tn(e_low, c_rows)
    total_t = jnp.exp(cum_t[:, CHUNK - 1 : CHUNK])
    for h in range(heads):
        part = slice(h * HEAD_DIM, (h + 1) * HEAD_DIM)
        state_grad[part, :] = total_t[h : h + 1, :] * r_now[part] + grown[part]

    d_pre_now = d_values * slope_x
    d_pre[0:CHUNK, :] = d_pre_now
    wide_out[4:5, :] += jnp.sum(d_pre_now, axis=0, keepdims=True)
    d_in = taps_ref[3:4, :inner] * d_pre_now
    wide_out[3:4, :] += jnp.sum(d_pre_now * conv_in[:, :inner], axis=0, keepdims=True)
    for k in range(3):
        earlier = extended[5 + k : 5 + k + CHUNK, :inner]
        wide_out[k : k + 1, :] += jnp.sum(d_pre_now * earlier, axis=0, keepdims=True)
        d_in = d_in + taps_ref[k : k + 1, :inner] * d_pre[3 - k : 3 - k + CHUNK, :]
    d_x_out[...] = d_in.astype(BF)
    d_pre[CHUNK : CHUNK + 8, :] = d_pre_now[0:8, :]


def weight_kernel(
    index_ref, x0, x1, x2, x3, g0, g1, g2, g3, gain_ref, w_ref, scaled_ref, d_gate_ref, d_x_ref,
    d_dt_ref, *rest,
):
    *sums_so_far, d_normed_out, total_out, dt_out = rest

    @pl.when(pl.program_id(0) == 0)
    def _():
        for i, ref in enumerate((total_out, dt_out)):
            ref[...] = sums_so_far[i][...] if sums_so_far else jnp.zeros(ref.shape, F32)

    _, _, normed = normed_blocks((x0, x1, x2, x3), gain_ref)
    d_wide = jnp.concatenate([d_gate_ref[...], d_x_ref[...]], axis=1)
    d_dt = d_dt_ref[...]
    d_all = jnp.concatenate([d_wide, d_dt], axis=1)
    scaled = scaled_ref[...]
    width = normed[0].shape[1]
    for k, (part, cot) in enumerate(zip(normed, (g0, g1, g2, g3))):
        rows = block_of(index_ref, k, width)
        total_out[rows, :] += dot_tn(part, d_wide)
        dt_out[rows, :] += dot_tn(part, d_dt)
        columns = slice(k * width, (k + 1) * width)
        total_out[4 * width :, columns] += dot_tn(scaled, cot[...])
        d_normed_out[:, k * width : (k + 1) * width] = dot_nn(d_all, w_ref[:, rows])


def mixed_kernel(
    index_ref, x0, x1, x2, x3, gain_ref, w_ref, d_act_ref, conv_ref, before_ref, taps_ref,
    d_normed_ref, own_out, send1, send2, send3, grad_out, taps_out, extended, d_pre,
):
    step_at = pl.program_id(0)
    chunk_at = pl.num_programs(0) - 1 - step_at
    own = conv_ref.shape[1]

    @pl.when(step_at == 0)
    def _():
        d_pre[CHUNK : CHUNK + 8, :] = jnp.zeros((8, own), F32)
        grad_out[...] = jnp.zeros(grad_out.shape, F32)
        taps_out[...] = jnp.zeros(taps_out.shape, F32)

    conv_in = conv_ref[...]
    extended[0:8, :] = jnp.where(chunk_at > 0, before_ref[...], 0.0)
    extended[8 : 8 + CHUNK, :] = conv_in
    pre_act = taps_ref[4:5, :] + taps_ref[3:4, :] * conv_in
    for k in range(3):
        pre_act = pre_act + taps_ref[k : k + 1, :] * extended[5 + k : 5 + k + CHUNK, :]
    d_pre_now = d_act_ref[...] * silu_slope(pre_act, sigmoid(pre_act))
    d_pre[0:CHUNK, :] = d_pre_now
    taps_out[4:5, :] += jnp.sum(d_pre_now, axis=0, keepdims=True)
    taps_out[3:4, :] += jnp.sum(d_pre_now * conv_in, axis=0, keepdims=True)
    d_in = taps_ref[3:4, :] * d_pre_now
    for k in range(3):
        earlier = extended[5 + k : 5 + k + CHUNK, :]
        taps_out[k : k + 1, :] += jnp.sum(d_pre_now * earlier, axis=0, keepdims=True)
        d_in = d_in + taps_ref[k : k + 1, :] * d_pre[3 - k : 3 - k + CHUNK, :]
    d_pre[CHUNK : CHUNK + 8, :] = d_pre_now[0:8, :]
    d_in = d_in.astype(BF)

    _, hats, normed = normed_blocks((x0, x1, x2, x3), gain_ref)
    width = normed[0].shape[1]
    row_dot = jnp.zeros((CHUNK, 1), F32)
    sends = (own_out, send1, send2, send3)
    for k, out in enumerate(sends):
        rows = block_of(index_ref, k, width)
        grad_out[rows, :] += dot_tn(normed[k], d_in)
        d_part = d_normed_ref[:, k * width : (k + 1) * width] + dot_nn(d_in, w_ref[:, rows])
        out[0, 0:CHUNK, :] = d_part.astype(out.dtype)
        scaled_hat = hats[k] * gain_ref[k : k + 1]
        row_dot = row_dot + jnp.sum(d_part * scaled_hat, axis=1, keepdims=True)
    dots = column_of_sums((row_dot,), 8)
    own_out[0, CHUNK : CHUNK + 8, :] = dots
    high, low = split2(dots)
    first = lax.broadcasted_iota(jnp.int32, (8, CHUNK), 0) == 0
    low = jnp.where(first, low.astype(F32), 0.0)
    low = jnp.concatenate([low[0:1], low[0:1], jnp.zeros((6, CHUNK), F32)], axis=0)
    high = high.astype(F32)
    both = jnp.where(first, high, low)
    both = jnp.concatenate([both, jnp.zeros((8, CHUNK), F32)], axis=0).astype(BF)
    for out in sends[1:]:
        out[0, CHUNK : CHUNK + 16, :] = both


def final_kernel(x0, x1, x2, x3, gain_ref, own_ref, r1, r2, r3, cot_ref, grad_out, gain_out):
    @pl.when(pl.program_id(0) == 0)
    def _():
        gain_out[...] = jnp.zeros(gain_out.shape, F32)

    blocks = [ref[...].astype(F32) for ref in (x0, x1, x2, x3)]
    inverse = inverse_rms(blocks)
    hat = blocks[0] * inverse
    received = [ref[0].astype(F32) for ref in (r1, r2, r3)]
    total = received[0] + received[1] + received[2]
    sums = own_ref[0, CHUNK : CHUNK + 8, :] + total[CHUNK : CHUNK + 8, :]
    sums = jnp.transpose(jnp.concatenate([sums, jnp.zeros((LANES - 8, CHUNK), F32)], axis=0))
    mean = (sums[:, 0:1] + sums[:, 1:2]) / (len(blocks) * hat.shape[1])
    d_own = own_ref[0, 0:CHUNK, :] + total[0:CHUNK]
    gain_out[0:1, :] += jnp.sum(d_own * hat, axis=0, keepdims=True)
    d_hat = d_own * gain_ref[0:1]
    grad = cot_ref[...].astype(F32) + inverse * (d_hat - hat * mean)
    grad_out[...] = grad
    top = jnp.max(jnp.abs(grad), axis=0, keepdims=True)
    gain_out[1:2, :] = jnp.maximum(gain_out[1:2, :], top)


def rows_spec(width, flip=None):
    if flip is None:
        return pl.BlockSpec((CHUNK, width), lambda c: (c, 0))
    return pl.BlockSpec((CHUNK, width), lambda c: (flip - 1 - c, 0))


def before_spec(width, count):
    ratio = CHUNK // 8
    return pl.BlockSpec((8, width), lambda c: (jnp.maximum((count - 1 - c) * ratio - 1, 0), 0))


def sums_spec(flip=None):
    if flip is None:
        return pl.BlockSpec((1, 8, CHUNK), lambda c: (c, 0, 0))
    return pl.BlockSpec((1, 8, CHUNK), lambda c: (flip - 1 - c, 0, 0))


def part_spec(more, width, flip=None):
    if flip is None:
        return pl.BlockSpec((1, CHUNK + more, width), lambda c: (c, 0, 0))
    return pl.BlockSpec((1, CHUNK + more, width), lambda c: (flip - 1 - c, 0, 0))


def whole_spec(shape):
    return pl.BlockSpec(shape, lambda c: (0,) * len(shape))


SCALARS = pl.BlockSpec(memory_space=pltpu.SMEM)


def call(kernel, name, chunks, in_specs, outs, scratch, flops, nbytes):
    return pl.pallas_call(
        kernel,
        name=name,
        grid=(chunks,),
        in_specs=in_specs,
        out_specs=[spec for spec, _, _ in outs],
        out_shape=[jax.ShapeDtypeStruct(shape, kind) for _, shape, kind in outs],
        scratch_shapes=scratch,
        compiler_params=pltpu.CompilerParams(
            dimension_semantics=("arbitrary",), vmem_limit_bytes=VMEM_LIMIT
        ),
        cost_estimate=pl.CostEstimate(flops=flops, bytes_accessed=nbytes, transcendentals=0),
    )


def swap(value, distance):
    count = lax.axis_size("head")
    return lax.ppermute(value, "head", [(i, i ^ distance) for i in range(count)])


def shift(value, axis, distance):
    count = lax.axis_size(axis)
    return lax.ppermute(value, axis, [(i, (i + distance) % count) for i in range(count)])


def pick(stack, position):
    return lax.dynamic_index_in_dim(stack, position, 0, keepdims=False)


def after(value, *earlier):
    return lax.optimization_barrier((value, earlier))[0]


def exchange(parts, z):
    shards = lax.axis_size("seq")
    pieces = [pick(parts, z)]
    for k in range(1, shards):
        pieces.append(shift(pick(parts, lax.rem(z + k, shards)), "seq", k))
    return pieces


def in_order(pieces, z, axis):
    size = pieces[0].shape[axis]
    count = len(pieces)
    ordered = jnp.concatenate(pieces[::-1] * 2, axis=axis)
    return lax.dynamic_slice_in_dim(ordered, (count - 1 - z) * size, count * size, axis)


def to_sequences(value, z):
    shards = lax.axis_size("seq")
    parts = value.reshape((shards, -1) + value.shape[1:])
    return in_order(exchange(parts, z), z, 1)


def to_tokens(value, z, top=None):
    shards = lax.axis_size("seq")
    parts = value.reshape(shards, value.shape[0] // shards, value.shape[1])
    if top is None:
        return in_order([piece[None] for piece in exchange(parts, z)], z, 0)
    power = exponent_of(top)
    pieces = [pick(parts, z)]
    for k in range(1, shards):
        payload = to_half(pick(parts, lax.rem(z + k, shards)), power)
        pieces.append(from_half(shift(payload, "seq", k))[0])
    return in_order([piece[None] for piece in pieces], z, 0)


def joined_tokens(parts):
    joined = jnp.stack(parts, axis=1)
    return joined.reshape((-1,) + joined.shape[2:])


def far_features(by_x, by_y):
    half = by_x.shape[0] // 2
    return jnp.concatenate([swap(by_x[:half], 2), swap(by_y[half:], 1)], axis=0)


HALF_TOP = 8.0


def exponent_of(top):
    return jnp.ceil(jnp.log2(jnp.maximum(top, 1e-30)))


def to_half(value, exponent):
    body = (value * jnp.exp2(HALF_TOP - exponent)).astype(jnp.float16)
    mark = jnp.full((16, value.shape[1]), exponent, F32).astype(jnp.float16)
    return jnp.concatenate([body, mark], axis=0)


def from_half(payload):
    exponent = payload[-1, 0].astype(F32)
    return payload[:-16].astype(F32) * jnp.exp2(exponent - HALF_TOP), exponent


def butterfly_sum(value):
    for axis in ("dp", "seq"):
        distance = 1
        while distance < lax.axis_size(axis):
            pairs = [(i, i ^ distance) for i in range(lax.axis_size(axis))]
            value = value + lax.ppermute(value, axis, pairs)
            distance *= 2
    return value


def on_device(
    hidden_in, norm_gain, w_z, w_x, w_bc, w_dt, conv_x, conv_x_bias, conv_bc, conv_bc_bias,
    dt_bias, a_log, skip, gate_gain, w_out, out_grad,
):
    shards = lax.axis_size("seq")
    z, me = lax.axis_index("seq"), lax.axis_index("head")
    length = hidden_in.shape[1] * shards
    part_width = hidden_in.shape[2]
    full_width = w_z.shape[0]
    inner = w_x.shape[1]
    heads = dt_bias.shape[0]
    bc_here = w_bc.shape[1]
    each = hidden_in.shape[0] // shards
    chunks = length // CHUNK
    conv_width = inner + 2 * STATE
    tail_width = conv_width + LANES
    index = jnp.bitwise_xor(me, jnp.arange(4, dtype=jnp.int32))

    hidden = to_sequences(hidden_in, z)

    largest = jnp.max(jnp.abs(w_out.astype(F32)))
    packed = jnp.concatenate(
        [
            w_bc.astype(F32),
            norm_gain.astype(F32).reshape(-1, bc_here),
            conv_bc,
            conv_bc_bias[None],
            jnp.full((1, bc_here), largest),
        ],
        axis=0,
    )
    packed = lax.all_gather(packed, "head")
    w_dt, w_bc, w_out = after((w_dt, w_bc, w_out), hidden)
    gain_end = full_width + part_width // bc_here
    w_bc_all = jnp.concatenate([packed[j, :full_width] for j in range(4)], axis=1).astype(BF)
    gain_all = packed[:, full_width:gain_end].reshape(4, part_width)
    gain_here = jnp.concatenate(
        [lax.dynamic_slice_in_dim(gain_all, index[k], 1, 0) for k in range(4)], axis=0
    )
    taps_bc_own = jnp.concatenate([conv_bc, conv_bc_bias[None], jnp.zeros((3, bc_here), F32)])
    taps_bc = jnp.concatenate([packed[j, gain_end : gain_end + 5] for j in range(4)], axis=1)
    out_scale = 16.0 / jnp.maximum(jnp.max(packed[:, gain_end + 5, 0]), 1e-30)
    taps_x = jnp.concatenate([conv_x, conv_x_bias[None]])
    taps = jnp.pad(jnp.concatenate([taps_x, taps_bc], axis=1), ((0, 3), (0, 0)))
    w_dt_wide = jnp.pad(w_dt, ((0, 0), (0, LANES - heads)))
    w_rest = jnp.concatenate([w_bc_all, w_dt_wide], axis=1)
    w_back = jnp.concatenate([w_z, w_x, w_dt_wide], axis=1).T
    w_bc_back = w_bc.T
    w_out_back = w_out.T
    w_out_parts = [
        lax.dynamic_slice_in_dim(w_out, index[k] * part_width, part_width, 1) for k in range(4)
    ]
    dt_params = jnp.pad(jnp.stack([dt_bias, a_log]), ((0, 6), (0, LANES - heads)))
    skip_wide = jnp.repeat(skip, HEAD_DIM)[None]
    gate_wide = gate_gain[None]
    owner = np.arange(inner) // HEAD_DIM
    spread = jnp.asarray(np.arange(LANES)[:, None] == owner[None, :], BF)
    collect = jnp.asarray(owner[:, None] == np.arange(LANES)[None, :], BF)
    order = np.arange(CHUNK)
    lower = jnp.asarray(order[:, None] >= order[None, :], BF)
    upper = jnp.asarray(order[:, None] <= order[None, :], BF)

    tokens = []
    near = [swap(hidden[0], 1), swap(hidden[0], 2)]
    pieces = exchange(after(out_grad, hidden).reshape((shards, each) + out_grad.shape[1:]), z)
    near, gain_here, w_rest, taps, w_out_back, w_back = after(
        (near, gain_here, w_rest, taps, w_out_back, w_back), hidden
    )
    near = after(near, gain_here, w_rest, taps, w_out_back, w_back)
    for s in range(each):
        own = hidden[s]
        if s:
            own = after(own, tokens[-1][3])
            near = [swap(own, 1), swap(own, 2)]
        tokens.append([own] + near + [far_features(*near)])
    straight = jnp.arange(4, dtype=jnp.int32)

    x_specs = [rows_spec(part_width)] * 4
    x_flipped = [rows_spec(part_width, chunks)] * 4
    g_specs = [
        pl.BlockSpec((None, CHUNK, part_width), lambda c, k=k: (k, c, 0)) for k in range(4)
    ]
    gain_spec = whole_spec((4, part_width))
    rows_inner = rows_spec(inner)

    forward = call(
        forward_kernel,
        "forward_scan",
        chunks,
        [SCALARS] + x_specs + [
            whole_spec(w_z.shape), whole_spec(w_x.shape), whole_spec(w_rest.shape), gain_spec,
            whole_spec(taps.shape), whole_spec((8, LANES)),
            whole_spec((1, inner)), whole_spec(spread.shape), whole_spec(lower.shape),
        ],
        [
            (rows_inner, (length, inner), F32),
            (rows_spec(tail_width), (length, tail_width), F32),
            (rows_inner, (length, inner), F32),
            (pl.BlockSpec((None, inner, STATE), lambda c: (c, 0, 0)), (chunks, inner, STATE), F32),
        ],
        [pltpu.VMEM((CHUNK + 8, conv_width), F32), pltpu.VMEM((inner, STATE), F32)],
        10**9, 10**7,
    )
    tokens[0] = after(tokens[0], tokens[-1][1:3])
    ahead = [
        forward(index, *x, w_z, w_x, w_rest, gain_here, taps, dt_params, skip_wide, spread, lower)
        for x in tokens
    ]
    own_cot = in_order(after(pieces, ahead[0][0], tokens[-1][1]), z, 1)
    own_cot = [own_cot[s] for s in range(each)]
    cotangents = [lax.all_gather(own, "head") for own in own_cot]

    score = call(
        score_kernel,
        "gate_sums",
        chunks,
        [SCALARS] + g_specs + [
            whole_spec(w_out_back.shape), rows_inner, rows_inner, whole_spec((1, inner)),
        ],
        [(rows_inner, (length, inner), F32), (sums_spec(), (chunks, 8, CHUNK), F32)],
        [],
        10**9, 10**6,
    )
    flipped = rows_spec(inner, chunks)
    backward = call(
        functools.partial(backward_kernel, inner * lax.axis_size("head")),
        "backward_scan",
        chunks,
        [SCALARS] + [sums_spec(chunks)] * 4 + [
            flipped, flipped, flipped, rows_spec(tail_width, chunks),
            before_spec(tail_width, chunks),
            pl.BlockSpec((None, inner, STATE), lambda c: (chunks - 1 - c, 0, 0)),
            whole_spec((1, inner)), whole_spec(taps.shape), whole_spec((8, LANES)),
            whole_spec((1, inner)), whole_spec(spread.shape), whole_spec(collect.shape),
            whole_spec(lower.shape), whole_spec(upper.shape),
        ],
        [
            (flipped, (length, inner), BF),
            (flipped, (length, inner), BF),
            (flipped, (length, inner), BF),
            (rows_spec(LANES, chunks), (length, LANES), BF),
            (rows_spec(2 * STATE, chunks), (length, 2 * STATE), F32),
            (whole_spec((8, inner)), (8, inner), F32),
            (whole_spec((8, LANES)), (8, LANES), F32),
        ],
        [
            pltpu.VMEM((CHUNK + 8, conv_width), F32),
            pltpu.VMEM((CHUNK + 8, inner), F32),
            pltpu.VMEM((inner, STATE), F32),
        ],
        2 * 10**9, 10**7,
    )
    sum_shapes = [(full_width + inner, full_width), (full_width, LANES)]

    def weigh(*args):
        return call(
            weight_kernel,
            "weight_sums",
            chunks,
            [SCALARS] + x_specs + g_specs + [
                gain_spec, whole_spec(w_back.shape), rows_inner, rows_inner, rows_inner,
                rows_spec(LANES),
            ] + [whole_spec(shape) for shape in sum_shapes[: len(args) - 15]],
            [(rows_spec(full_width), (length, full_width), F32)]
            + [(whole_spec(shape), shape, F32) for shape in sum_shapes],
            [],
            2 * 10**9, 10**7,
        )(*args)

    mix = call(
        mixed_kernel,
        "input_sums",
        chunks,
        [SCALARS] + x_flipped + [gain_spec, whole_spec(w_bc_back.shape)]
        + [rows_spec(bc_here, chunks)] * 2
        + [before_spec(bc_here, chunks), whole_spec((8, bc_here)), rows_spec(full_width, chunks)],
        [
            (part_spec(8, part_width, chunks), (chunks, CHUNK + 8, part_width), F32),
            (part_spec(16, part_width, chunks), (chunks, CHUNK + 16, part_width), BF),
            (part_spec(16, part_width, chunks), (chunks, CHUNK + 16, part_width), BF),
            (part_spec(16, part_width, chunks), (chunks, CHUNK + 16, part_width), BF),
            (whole_spec((full_width, bc_here)), (full_width, bc_here), F32),
            (whole_spec((8, bc_here)), (8, bc_here), F32),
        ],
        [pltpu.VMEM((CHUNK + 8, bc_here), F32), pltpu.VMEM((CHUNK + 8, bc_here), F32)],
        10**9, 10**7,
    )
    finish = call(
        final_kernel,
        "input_gradient",
        chunks,
        x_specs + [gain_spec, part_spec(8, part_width)] + [part_spec(16, part_width)] * 3
        + [rows_spec(part_width)],
        [
            (rows_spec(part_width), (length, part_width), F32),
            (whole_spec((8, part_width)), (8, part_width), F32),
        ],
        [],
        10**8, 10**6,
    )

    def scores_of(s, cotangent):
        gate, _, ssd, _ = ahead[s]
        d_scaled, sums = score(straight, *[cotangent] * 4, w_out_back, ssd, gate, gate_wide)
        return d_scaled, [sums] + [swap(sums, k) for k in range(1, 4)]

    def d_bc_sends(d_bc):
        power = exponent_of(jnp.max(jnp.abs(d_bc)))
        parts = [
            lax.dynamic_slice_in_dim(d_bc, index[k] * bc_here, bc_here, 1) for k in range(4)
        ]
        payloads = [
            to_half(jnp.concatenate([p[: length // 2], p[length // 2 :]], axis=1), power)
            for p in parts[1:]
        ]
        return parts[0], payloads

    def d_bc_total(own, payloads):
        total = sum(from_half(swap(part, k + 1))[0] for k, part in enumerate(payloads))
        return own + jnp.concatenate([total[:, :bc_here], total[:, bc_here:]], axis=0)

    behind, d_bc_all = [], []
    for s in range(each):
        gate, conv, ssd, states = ahead[s]
        cotangent = after(cotangents[s], behind[-1][0]) if behind else cotangents[s]
        d_scaled, sums = scores_of(s, cotangent)
        if behind:
            own, payloads = d_bc_sends(behind[-1][4])
            sums = after(sums, payloads)
            d_bc_all.append(d_bc_total(own, payloads))
        behind.append(
            backward(
                index, *sums, ssd, gate, d_scaled, conv, conv, states, gate_wide, taps, dt_params,
                skip_wide, spread, collect, lower, upper,
            )
        )

    g_sums, mixed, d_normed_all = [], [], []
    for s in range(each):
        scaled, d_gate, d_x, d_dt, _, _, _ = behind[s]
        d_dt = after(d_dt, behind[-1][0])
        d_normed, *g_sums = weigh(
            index, *tokens[s], *[cotangents[s]] * 4, gain_here, w_back, scaled, d_gate, d_x, d_dt,
            *g_sums,
        )
        d_normed_all.append(d_normed)
    g_total, g_dt = g_sums
    g_total_sum = lax.psum(g_total, ("seq", "dp"))

    d_bc_all.append(d_bc_total(*d_bc_sends(after(behind[-1][4], g_total))))
    for s in range(each):
        d_normed = after(d_normed_all[s], g_total, [part[0] for part in mixed])
        conv_own = lax.dynamic_slice_in_dim(ahead[s][1], inner + me * bc_here, bc_here, 1)
        own, send1, send2, send3, g_bc, taps_sums = mix(
            index, *tokens[s], gain_here, w_bc_back, d_bc_all[s], conv_own, conv_own, taps_bc_own,
            d_normed,
        )
        mixed.append((own, (swap(send1, 1), swap(send2, 2), swap(send3, 3)), g_bc, taps_sums))
    blocks = []
    for s in range(each):
        scaled = after(behind[s][0], mixed[-1][0])
        out_parts = [jnp.dot(scaled, part, preferred_element_type=F32) for part in w_out_parts]
        sent = [(out_parts[k] * out_scale).astype(jnp.float16) for k in range(1, 4)]
        received = [swap(part, k + 1) for k, part in enumerate(after(sent, mixed[s][1]))]
        block = tokens[s][0].astype(F32) + out_parts[0]
        blocks.append((block + sum(part.astype(F32) for part in received) / out_scale).astype(BF))
    sent_blocks = [to_tokens(block, z) for block in blocks]
    wide = sum(part[5] for part in behind)
    dt_sums = sum(part[6] for part in behind)

    grads, gain_sums = [], []
    for s in range(each):
        own, sends, _, _ = mixed[s]
        own = after(own, mixed[-1][0])
        grad, gain_sum = finish(*tokens[s], gain_here, own, *sends, own_cot[s])
        gain_sums.append(gain_sum[0:1])
        grads.append(to_tokens(grad, z, jnp.max(gain_sum[1])))
    g_bc = sum(part[2] for part in mixed)
    taps_sums = sum(part[3] for part in mixed)
    gain_sums = sum(gain_sums)
    late = [
        part.reshape(-1, LANES)
        for part in (g_bc, g_dt[:, :heads], wide, dt_sums, taps_sums, gain_sums)
    ]
    ends = np.cumsum([0] + [part.shape[0] for part in late])
    late = butterfly_sum(jnp.concatenate(late, axis=0))
    late = [late[ends[i] : ends[i + 1]] for i in range(len(ends) - 1)]
    g_bc, g_dt, wide, dt_sums, taps_sums, gain_sums = late
    g_bc = g_bc.reshape(full_width, bc_here)
    g_dt = g_dt.reshape(full_width, heads)
    wide = wide.reshape(8, inner)
    taps_sums = taps_sums.reshape(8, bc_here)
    gain_sums = gain_sums.reshape(1, part_width)
    return (
        joined_tokens(sent_blocks),
        joined_tokens(grads),
        gain_sums[0],
        g_total_sum[:full_width, :inner],
        g_total_sum[:full_width, inner:],
        g_bc,
        g_dt,
        wide[0:4],
        wide[4],
        taps_sums[0:4],
        taps_sums[4],
        dt_sums[1, :heads],
        dt_sums[0, :heads],
        wide[6].reshape(heads, HEAD_DIM).sum(axis=1),
        wide[5],
        g_total_sum[full_width:],
    )


def fits(mesh, seqs, length):
    shards = mesh.shape["seq"]
    local_seqs = seqs // mesh.shape["dp"]
    doubling = all(mesh.shape[axis] & (mesh.shape[axis] - 1) == 0 for axis in ("seq", "dp"))
    return doubling and mesh.shape["head"] == 4 and local_seqs % shards == 0 and length % CHUNK == 0


def solution(mesh):
    in_specs = (
        P("dp", "seq", "head"),
        P("head"),
        P(None, "head"),
        P(None, "head"),
        P(None, "head"),
        P(None, "head"),
        P(None, "head"),
        P("head"),
        P(None, "head"),
        P("head"),
        P("head"),
        P("head"),
        P("head"),
        P("head"),
        P("head", None),
        P("dp", "seq", "head"),
    )
    out_specs = (
        P("dp", "seq", "head"),
        P("dp", "seq", "head"),
        P("head"),
        P(None, "head"),
        P(None, "head"),
        P(None, "head"),
        P(None, "head"),
        P(None, "head"),
        P("head"),
        P(None, "head"),
        P("head"),
        P("head"),
        P("head"),
        P("head"),
        P("head"),
        P("head", None),
    )

    def run(*args):
        seqs, length, _ = args[0].shape
        body = on_device if fits(mesh, seqs, length) else on_device_general
        return jax.shard_map(
            body, mesh=mesh, in_specs=in_specs, out_specs=out_specs, check_vma=False
        )(*args)

    return run
```
